32 devices in a mesh: blk: 4 (over y, x), grp: 8 (over z, core).
Axes of the slice: x: 2, y: 2, z: 4, core: 2. Of those that a mesh axis runs over, the one named last changes fastest.
Arguments:
- incident: float32 [4, 8192, 240], P('blk', 'grp'), may hold values from -6 to 6
- mie_coef: float32 [4, 8192, 240], P('blk', 'grp'), may hold values from 0.15 to 0.45
- owner_dev: int32 [4, 24576, 1], P('blk', 'grp'), may hold values from 0 to 7; in each aligned block of 3072 rows (0 to 3071, 3072 to 6143, ..., all dimensions but the last counted through in order) at most 512 rows name the same one
- near_row: int32 [4, 24576], P('blk', 'grp'), may hold values from 0 to 1023
- table_id: int32 [4, 24576], P('blk', 'grp'), may hold values from 0 to 7
- tables: bfloat16 [8, 240, 240], replicated, may hold values from -0.4 to 0.6
- wave_out: bfloat16 [240, 512], replicated, may hold values from -0.375 to 0.375
- wave_in: bfloat16 [512, 240], replicated, may hold values from -0.25 to 0.25
- plane_angle: bfloat16 [4, 8192, 512], P('blk', 'grp'), may hold values from -3.140625 to 3.140625
- far_trans: float32 [4, 8, 4, 512], P('blk', 'grp'), may hold values from -0.109375 to 0.109375
Outputs:
- solution: float32 [4, 8192, 240], P('blk', 'grp')
- residual: float32 [4, 8192, 240], P('blk', 'grp')
- hessenberg: float32 [3, 2], replicated
The draws below stay inside these ranges and needn't reach their ends.
Inputs may be any that keep to these rules, and one draw needn't show every extreme that they name: `owner_dev`: among the 3072 requests of one device, at most 512 name the same owner, and some device reaches 512.
All inputs are finite; a program needn't handle non-finite values.
Results may differ from the reference program's by a relative error of at most 0.0075.
Values may be sent and summed in bfloat16 or wider, within the bound.
No kernel may reach another device: no remote copies, remote signals or barrier semaphores. Data moves between devices by JAX's collectives and lax.ppermute only.
A program may use at most 128 MiB of HBM per device.

```python
import math
import jax
import jax.numpy as jnp
import numpy as np
from jax import lax

C = 240
M = 512
NTAB = 8
K = 3
P_SIZE = 1024
CAP = 512
Q = 3072
GROUP_ROWS = 8192
GROUP_REQ = 24576
N_BLK = 4
N_GRP = 8


def draw_incident(key, part):
    key_common = jax.random.fold_in(key, 11)
    key_noise = jax.random.fold_in(key, 12)
    total_rows = N_BLK * GROUP_ROWS
    position = jnp.arange(total_rows, dtype=jnp.int32).astype(jnp.float32) / (1.0 * (total_rows - 1))
    position = position.reshape(N_BLK, GROUP_ROWS, 1)
    common = jax.random.normal(key_common, (1, 1, C), jnp.float32)
    noise = 0.5 * jax.random.normal(key_noise, (N_BLK, GROUP_ROWS, C), jnp.float32)
    ramp = 0.4 + 1.2 * position
    return jnp.clip(ramp * (common + noise), -6.0, 6.0)


def draw_mie_coef(key, part):
    key_mie = jax.random.fold_in(key, 21)
    unit = jax.random.uniform(key_mie, (N_BLK, GROUP_ROWS, C), jnp.float32, -1.0, 1.0)
    return 0.3 + 0.15 * unit


def draw_tables(key, part):
    key_shared = jax.random.fold_in(key, 31)
    key_own = jax.random.fold_in(key, 32)
    shared = jax.random.normal(key_shared, (C, C), jnp.float32)
    own = jax.random.normal(key_own, (NTAB, C, C), jnp.float32)
    symmetric = (shared + shared.T) * (0.25 / math.sqrt(2.0 * C))
    identity = jnp.eye(C, dtype=jnp.float32)
    tables = 0.3 * identity[None] + symmetric[None] + own * (0.5 / math.sqrt(1.0 * C))
    return jnp.clip(tables, -0.4, 0.6).astype(jnp.bfloat16)


def plant(drawn, rng, low, high):
    dims = drawn.shape
    spot = [jax.random.randint(jax.random.fold_in(rng, axis), (), 0, dims[axis]) for axis in range(len(dims))]
    drawn = drawn.at[tuple(spot)].set(low)
    longest = dims.index(max(dims))
    spot[longest] = (spot[longest] + 1) % dims[longest]
    return drawn.at[tuple(spot)].set(high)


def levels(own_key, extent, shards, least, top_value):
    gain, own = 1.0, jax.random.fold_in(own_key, 6)
    for dim, parts in shards:
        steps = jnp.exp(jax.random.uniform(jax.random.fold_in(own, dim), (parts,), jnp.float32, least / len(shards), top_value / len(shards)))
        gain = gain * jnp.repeat(steps, extent[dim] // parts).reshape([-1 if axis == dim else 1 for axis in range(len(extent))])
    return gain


def assign_block(stream_key, own, number, rows, amount, top, most, lean):
    order = jax.random.permutation(stream_key, amount)
    heavy_load, usual = shares(amount, rows * top, most, lean, True), shares(amount, rows * top, most, lean, False)
    places = jnp.arange(amount)

    def named(lengths, rotation):
        used = int((lengths > 0).sum())
        fixed = max(1, used // 4)
        shifted = fixed + (places - fixed + rotation * (used - fixed)) % max(1, amount - fixed)
        return jnp.zeros((amount,), jnp.int32).at[order[jnp.where(places < fixed, places, shifted)]].set(jnp.asarray(lengths, jnp.int32))

    lengths = jnp.where(number % 4 == 0, named(heavy_load, number // 4), named(usual, number - number // 4 - 1))
    mixed = jax.random.permutation(jax.random.fold_in(own, 3), amount)
    donor, taker = mixed[0:amount // 2 * 2:2], mixed[1:amount // 2 * 2:2]
    slack = jnp.minimum(lengths[donor] - 1, most - lengths[taker]) // 2
    slack = jnp.where((donor == order[0]) | (taker == order[0]) | (lengths[taker] == 0), 0, jnp.maximum(slack, 0))
    shifted = jax.random.randint(jax.random.fold_in(own, 4), (amount // 2,), 0, 1 << 20) % (slack + 1)
    lengths = lengths.at[donor].add(-shifted).at[taker].add(shifted)
    members = jnp.searchsorted(jnp.cumsum(lengths), jnp.arange(rows * top), side="right").astype(jnp.int32)
    table = members.reshape(top, rows).T
    table = table[jax.random.permutation(jax.random.fold_in(own, 1), rows)]
    rotation = jax.random.randint(jax.random.fold_in(own, 2), (rows, 1), 0, top)
    return jnp.take_along_axis(table, (jnp.arange(top)[None, :] + rotation) % top, axis=1)


def shares(amount, total, limit, slope, full):
    weights = [(1 << 20) // math.isqrt(grade ** slope) + 1 for grade in range(1, amount + 1)]
    largest = limit if full else min(limit, max(-(-total // amount), total * weights[0] // sum(weights)))
    least = 1 if total - largest >= amount - 1 else 0
    holding, surplus = [largest] + [least] * (amount - 1), total - largest - least * (amount - 1)
    while surplus > 0:
        free = [i for i in range(1, amount) if holding[i] < largest] or [i for i in range(1, amount) if holding[i] < limit]
        mass, budget = sum([weights[i] for i in free]), surplus
        for i in free:
            extra = min(limit - holding[i], max(1, budget * weights[i] // mass), surplus)
            holding[i] = holding[i] + extra
            surplus = surplus - extra
    return np.array(holding)


def gaussian(rng, shape, scale, bound, split=(), held_as=jnp.bfloat16):
    values = scale * jax.random.normal(rng, shape, jnp.float32)
    if split:
        values = values * levels(rng, shape, split, -0.22, 0.18)
    return jnp.clip(values, -bound, bound).astype(held_as)


def setup_inputs(seed: int = 0) -> dict:
    key_of = jax.random.split(jax.random.key(seed), 11)
    incident = draw_incident(jax.random.fold_in(key_of[10], 71), 0)
    mie_coef = draw_mie_coef(jax.random.fold_in(key_of[10], 71), 0)
    owner_dev_keys = jax.random.split(jax.random.fold_in(key_of[2], 1), N_BLK * GROUP_REQ // Q)
    owner_dev_turns = jax.random.permutation(jax.random.fold_in(key_of[2], 3), N_BLK * GROUP_REQ // Q)
    owner_dev = jax.vmap(lambda own, number: assign_block(jax.random.fold_in(key_of[2], 2), own, number, Q, N_GRP, 1, CAP, 2))(owner_dev_keys, owner_dev_turns).reshape((N_BLK, GROUP_REQ, 1))
    near_row = plant(jax.random.randint(key_of[3], (N_BLK, GROUP_REQ), 0, P_SIZE), jax.random.fold_in(key_of[3], 1), 0, P_SIZE - 1).astype(jnp.int32)
    table_id = plant(jax.random.randint(key_of[4], (N_BLK, GROUP_REQ), 0, NTAB), jax.random.fold_in(key_of[4], 1), 0, NTAB - 1).astype(jnp.int32)
    tables = draw_tables(jax.random.fold_in(key_of[10], 71), 0)
    wave_out = gaussian(key_of[6], (C, M), C ** -0.5, 0.375)
    wave_in = gaussian(key_of[7], (M, C), M ** -0.5, 0.25)
    plane_angle = jnp.clip(jax.random.uniform(key_of[8], (N_BLK, GROUP_ROWS, M), jnp.float32, -3.140625, 3.140625), -3.140625, 3.140625).astype(jnp.bfloat16)
    far_trans = gaussian(key_of[9], (N_BLK, N_GRP, N_BLK, M), (P_SIZE * (N_BLK - 1)) ** -0.5, 0.109375, ((0, 4), (1, 8)), jnp.float32)
    return {"incident": incident, "mie_coef": mie_coef, "owner_dev": owner_dev, "near_row": near_row, "table_id": table_id, "tables": tables, "wave_out": wave_out, "wave_in": wave_in, "plane_angle": plane_angle, "far_trans": far_trans}


epsilon = 1e-06

def apply_operator(vector, mie_coef, source_ids, table_id, tables, wave_out, wave_in, cosine, far_trans):
    block_count, group_rows, coef_count = vector.shape
    coded = vector.astype(jnp.bfloat16).astype(jnp.float32)
    flat_coded = coded.reshape(-1, coef_count)
    near_terms = jnp.zeros((block_count, source_ids.shape[1], coef_count), jnp.float32)
    for table_index in range(NTAB):
        translated = jnp.dot(flat_coded, tables[table_index].astype(jnp.float32), precision=lax.Precision.HIGHEST).reshape(vector.shape)
        translated = translated.astype(jnp.bfloat16).astype(jnp.float32)
        fetched = jax.vmap(lambda rows_all, wanted: rows_all[wanted])(translated, source_ids)
        near_terms = near_terms + jnp.where((table_id == table_index)[:, :, None], fetched, 0.0)
    near_field = near_terms.reshape(block_count, group_rows, K, coef_count).sum(axis=2)
    outgoing = jnp.dot(flat_coded, wave_out.astype(jnp.float32), precision=lax.Precision.HIGHEST).reshape(block_count, group_rows, M)
    gathered = (cosine * outgoing).reshape(block_count, N_GRP, P_SIZE, M).sum(axis=2)
    far_mask = 1.0 - jnp.eye(block_count, dtype=jnp.float32)
    incoming = jnp.einsum('bgcm,bc,cgm->bgm', far_trans, far_mask, gathered, precision=lax.Precision.HIGHEST)
    spread = (cosine * jnp.repeat(incoming, P_SIZE, axis=1)).astype(jnp.bfloat16).astype(jnp.float32)
    far_field = jnp.dot(spread.reshape(-1, M), wave_in.astype(jnp.float32), precision=lax.Precision.HIGHEST).reshape(vector.shape)
    return vector - mie_coef * (near_field + far_field)

def reference(incident, mie_coef, owner_dev, near_row, table_id, tables, wave_out, wave_in, plane_angle, far_trans):
    source_ids = (owner_dev[:, :, 0] * P_SIZE + near_row).astype(jnp.int32)
    cosine = jnp.cos(plane_angle.astype(jnp.float32))

    def operator(vector):
        return apply_operator(vector, mie_coef, source_ids, table_id, tables, wave_out, wave_in, cosine, far_trans)
    initial_norm = jnp.sqrt(jnp.sum(incident * incident) + epsilon)
    first_basis = incident / initial_norm
    first_image = operator(first_basis)
    diag_first = jnp.sum(first_basis * first_image)
    resid_first = first_image - diag_first * first_basis
    below_first = jnp.sqrt(jnp.sum(resid_first * resid_first) + epsilon)
    second_basis = resid_first / below_first
    second_image = operator(second_basis)
    upper_second = jnp.sum(first_basis * second_image)
    diag_second = jnp.sum(second_basis * second_image)
    resid_second = second_image - upper_second * first_basis - diag_second * second_basis
    below_second = jnp.sqrt(jnp.sum(resid_second * resid_second) + epsilon)
    gram_aa = diag_first * diag_first + below_first * below_first
    gram_ab = diag_first * upper_second + below_first * diag_second
    gram_bb = upper_second * upper_second + diag_second * diag_second + below_second * below_second
    rhs_first = initial_norm * diag_first
    rhs_second = initial_norm * upper_second
    determinant = gram_aa * gram_bb - gram_ab * gram_ab
    coef_first = (gram_bb * rhs_first - gram_ab * rhs_second) / determinant
    coef_second = (gram_aa * rhs_second - gram_ab * rhs_first) / determinant
    solution = coef_first * first_basis + coef_second * second_basis
    residual = incident - coef_first * first_image - coef_second * second_image
    zero_entry = jnp.zeros((), jnp.float32)
    hessenberg = jnp.stack([jnp.stack([diag_first, upper_second]), jnp.stack([below_first, diag_second]), jnp.stack([zero_entry, below_second])])
    return (solution, residual, hessenberg)
```

```python
import functools

import jax
import jax.numpy as jnp
import numpy as np
from jax import lax
from jax.experimental import pallas as pl
from jax.experimental.pallas import tpu as pltpu
from jax.sharding import PartitionSpec as P

epsilon = 1e-06
LANES = 128
CHUNK = 256
BATCH = 32
VMEM_LIMIT = 56 * 2**20


def cosine_coefficients():
    top = 3.1416**2
    nodes = (np.cos((np.arange(400) + 0.5) * np.pi / 400) + 1.0) * top / 2.0
    fit = np.polynomial.chebyshev.Chebyshev.fit(nodes, np.cos(np.sqrt(nodes)), 8, domain=[0.0, top])
    return [float(c) for c in fit.convert(kind=np.polynomial.Polynomial).coef]


COS = cosine_coefficients()


def cosine(angle):
    square = angle * angle
    value = jnp.full_like(square, COS[-1])
    for coef in COS[-2::-1]:
        value = value * square + coef
    return value


def whole(memory=pltpu.VMEM):
    return pl.BlockSpec(memory_space=memory)


def params():
    return pltpu.CompilerParams(vmem_limit_bytes=VMEM_LIMIT)


def pad_lanes(value, width):
    rows, cols = value.shape
    return jnp.concatenate([value, jnp.zeros((rows, width - cols), value.dtype)], axis=1)


def code_kernel(field_ref, coded_ref):
    coefs, rows = field_ref.shape
    width = coded_ref.shape[1]
    for start in range(0, rows, CHUNK):
        part = field_ref[:, pl.ds(start, CHUNK)]
        part = jnp.concatenate([part, jnp.zeros((width - coefs, CHUNK), part.dtype)], axis=0)
        coded_ref[pl.ds(start, CHUNK), :] = part.T.astype(jnp.bfloat16)


def code(field_t, width):
    rows = field_t.shape[1]
    return pl.pallas_call(
        code_kernel,
        out_shape=jax.ShapeDtypeStruct((rows, width), jnp.bfloat16),
        in_specs=[whole()],
        out_specs=whole(),
        compiler_params=params(),
        name="code_rows",
    )(field_t)


def wave_kernel(coded_ref, out_ref, angle_ref, sum_ref):
    coefs, samples = out_ref.shape
    rows = coded_ref.shape[0]

    def part(index, total):
        at = pl.ds(pl.multiple_of(index * CHUNK, CHUNK), CHUNK)
        outgoing = jnp.dot(
            coded_ref[at, :][:, :coefs], out_ref[...], preferred_element_type=jnp.float32
        )
        weighted = cosine(angle_ref[at, :].astype(jnp.float32)) * outgoing
        return total + jnp.sum(weighted, axis=0, keepdims=True)

    sum_ref[...] = lax.fori_loop(0, rows // CHUNK, part, jnp.zeros((1, samples), jnp.float32))


def gather_wave(coded, wave_out, angle):
    rows, samples = angle.shape
    return pl.pallas_call(
        wave_kernel,
        out_shape=jax.ShapeDtypeStruct((1, samples), jnp.float32),
        in_specs=[whole()] * 3,
        out_specs=whole(),
        compiler_params=params(),
        cost_estimate=pl.CostEstimate(
            flops=2 * rows * samples * 256, bytes_accessed=2 * 2**20, transcendentals=0
        ),
        name="gather_wave",
    )(coded, wave_out, angle)


def spread_kernel(incoming_ref, in_ref, angle_ref, far_ref):
    rows = angle_ref.shape[0]

    def part(index, carry):
        at = pl.ds(pl.multiple_of(index * CHUNK, CHUNK), CHUNK)
        spread = cosine(angle_ref[at, :].astype(jnp.float32)) * incoming_ref[...]
        far_ref[at, :] = lax.dot_general(
            spread.astype(jnp.bfloat16),
            in_ref[...],
            (((1,), (1,)), ((), ())),
            preferred_element_type=jnp.float32,
        )
        return carry

    lax.fori_loop(0, rows // CHUNK, part, 0)


def spread_wave(incoming, wave_in_t, angle):
    rows, samples = angle.shape
    coefs = wave_in_t.shape[0]
    return pl.pallas_call(
        spread_kernel,
        out_shape=jax.ShapeDtypeStruct((rows, coefs), jnp.float32),
        in_specs=[whole()] * 3,
        out_specs=whole(),
        compiler_params=params(),
        cost_estimate=pl.CostEstimate(
            flops=2 * rows * samples * 256, bytes_accessed=3 * 2**20, transcendentals=0
        ),
        name="spread_wave",
    )(incoming, wave_in_t, angle)


def near_kernel(groups, second, slot_ref, table_ref, tables_ref, vec_ref, mie_ref, far_ref, *rest):
    if second:
        first_ref, sums_in_ref, *rest = rest
    count = sum(groups)
    shards, (image_ref, other_ref, sums_ref, source, picked) = rest[:count], rest[count:]
    rows, coefs = vec_ref.shape
    requests = slot_ref.shape[0]
    per_row = requests // rows
    width = 2 * LANES
    first = 0
    for place, members in enumerate(groups):
        value = shards[first][...].astype(jnp.float32)
        for member in range(1, members):
            value = value + shards[first + member][...].astype(jnp.float32)
        first += members
        base = place * 2 * rows
        source[pl.ds(base, rows, stride=2), :] = value[:, :LANES]
        source[pl.ds(base + 1, rows, stride=2), :] = value[:, LANES:]

    def pick(step, carry):
        start = pl.multiple_of(step * BATCH, BATCH)
        got = [
            source[pl.ds(pl.multiple_of(slot_ref[start + k], 2), 2), :] for k in range(BATCH)
        ]
        for k in range(0, BATCH, 4):
            picked[pl.ds(pl.multiple_of(2 * (start + k), 8), 8), :] = jnp.concatenate(
                got[k : k + 4], axis=0
            )
        return carry

    lax.fori_loop(0, requests // BATCH, pick, 0)

    def part(index, sums):
        start = pl.multiple_of(index * CHUNK, CHUNK)
        at = pl.ds(start, CHUNK)
        stride = 2 * per_row
        halves = [
            [
                picked[pl.ds(start * stride + 2 * k + h, CHUNK, stride=stride), :].astype(
                    jnp.bfloat16
                )
                for h in range(2)
            ]
            for k in range(per_row)
        ]
        named = [
            jnp.broadcast_to(table_ref[at, k : k + 1], (CHUNK, LANES)).astype(jnp.bfloat16)
            for k in range(per_row)
        ]
        zero = jnp.zeros((CHUNK, LANES), jnp.bfloat16)
        near = jnp.zeros((CHUNK, coefs), jnp.float32)
        for t in range(tables_ref.shape[0]):
            chosen = [named[k] == jnp.bfloat16(t) for k in range(per_row)]
            mixed = []
            for h in range(2):
                value = jnp.where(chosen[0], halves[0][h], zero)
                for k in range(1, per_row):
                    value = value + jnp.where(chosen[k], halves[k][h], zero)
                mixed.append(value)
            near = near + jnp.dot(
                jnp.concatenate(mixed, axis=1)[:, :coefs],
                tables_ref[t],
                preferred_element_type=jnp.float32,
            )
        vec = vec_ref[at, :]
        image = vec - mie_ref[at, :] * (near + far_ref[at, :])

        def dot(a, b):
            return jnp.sum(a * b, axis=0, keepdims=True)

        if second:
            image_ref[:, at] = pad_lanes(image, width).T[:coefs, :]
            new = [dot(first_ref[at, :], image), dot(vec, image), dot(image, image)]
        else:
            image_ref[at, :] = image
            other_ref[at, :] = pad_lanes(image, width).astype(jnp.bfloat16)
            new = [dot(vec, vec), dot(vec, image), dot(image, image)]
        return tuple(a + b for a, b in zip(sums, new, strict=True))

    sums = lax.fori_loop(
        0, rows // CHUNK, part, tuple(jnp.zeros((1, coefs), jnp.float32) for _ in range(3))
    )
    lane = lax.broadcasted_iota(jnp.int32, (1, LANES), 1)
    packed = sums_in_ref[...] if second else jnp.zeros((1, LANES), jnp.float32)
    for k, value in enumerate(sums):
        total = jnp.sum(value, axis=1, keepdims=True)
        packed = jnp.where(lane == k + (3 if second else 0), total, packed)
    sums_ref[...] = jnp.broadcast_to(packed, sums_ref.shape)


def near_field(groups, slots, table_ids, tables, vec, mie, far, shards, second=None, devices=1):
    rows, coefs = vec.shape
    requests = slots.shape[0]
    width = 2 * LANES
    extra = () if second is None else second
    if second is None:
        outs = (
            jax.ShapeDtypeStruct((rows, coefs), jnp.float32),
            jax.ShapeDtypeStruct((rows, width), jnp.bfloat16),
            jax.ShapeDtypeStruct((1, LANES), jnp.float32),
        )
    else:
        outs = (
            jax.ShapeDtypeStruct((coefs, rows), jnp.float32),
            jax.ShapeDtypeStruct((8, LANES), jnp.float32),
            jax.ShapeDtypeStruct((devices, LANES), jnp.float32),
        )
    return pl.pallas_call(
        functools.partial(near_kernel, groups, second is not None),
        out_shape=outs,
        in_specs=[whole(pltpu.SMEM)] + [whole()] * (5 + len(extra) + len(shards)),
        out_specs=(whole(),) * 3,
        scratch_shapes=[
            pltpu.VMEM((len(groups) * rows * 2, LANES), jnp.float32),
            pltpu.VMEM((requests * 2, LANES), jnp.float32),
        ],
        compiler_params=params(),
        cost_estimate=pl.CostEstimate(
            flops=2 * rows * 8 * 256 * 256, bytes_accessed=10 * 2**20, transcendentals=0
        ),
        name="near_second" if second is not None else "near_first",
    )(slots, table_ids, tables, vec, mie, far, *extra, *shards)


def finish_kernel(sums_ref, x_ref, u_ref, v_ref, solution_ref, residual_ref, hess_ref):
    sums = jnp.sum(sums_ref[...], axis=0, keepdims=True)
    xx, xu, uu, xv, uv, vv = [sums[:, k : k + 1] for k in range(6)]
    norm = jnp.sqrt(xx + epsilon)
    inverse = 1.0 / norm
    squared = inverse * inverse
    h11 = xu * squared
    ones = xx * squared
    size1 = uu * squared - 2.0 * h11 * h11 + h11 * h11 * ones
    h21 = jnp.sqrt(jnp.maximum(size1, 0.0) + epsilon)
    q = inverse / h21
    h12 = q * inverse * (xv - h11 * xu)
    h22 = q * q * (uv - h11 * uu - h11 * xv + h11 * h11 * xu)
    size2 = q * q * (vv - 2.0 * h11 * uv + h11 * h11 * uu)
    cross = q * inverse * (xu - h11 * xx)
    twos = size1 / (h21 * h21)
    left = (
        size2
        - 2.0 * h12 * h12
        - 2.0 * h22 * h22
        + h12 * h12 * ones
        + h22 * h22 * twos
        + 2.0 * h12 * h22 * cross
    )
    h32 = jnp.sqrt(jnp.maximum(left, 0.0) + epsilon)
    gram00 = h11 * h11 + h21 * h21
    gram01 = h11 * h12 + h21 * h22
    gram11 = h12 * h12 + h22 * h22 + h32 * h32
    rhs0, rhs1 = norm * h11, norm * h12
    det = gram00 * gram11 - gram01 * gram01
    y1 = (gram11 * rhs0 - gram01 * rhs1) / det
    y2 = (gram00 * rhs1 - gram01 * rhs0) / det
    x, u, v = x_ref[...], u_ref[...], v_ref[...]
    a1, a2 = y1 * inverse, y2 * q
    solution_ref[...] = (a1 - h11 * a2) * x + a2 * u
    residual_ref[...] = x - (a1 - h11 * a2) * u - a2 * v
    hess_ref[0:1, 0:1] = h11
    hess_ref[0:1, 1:2] = h21
    hess_ref[0:1, 2:3] = jnp.zeros_like(h11)
    hess_ref[1:2, 0:1] = h12
    hess_ref[1:2, 1:2] = h22
    hess_ref[1:2, 2:3] = h32


def finish(sums, x_t, u_t, v_t):
    coefs, rows = x_t.shape
    part = 48 if coefs % 48 == 0 else coefs
    block = pl.BlockSpec((part, rows), lambda i: (i, 0))
    return pl.pallas_call(
        finish_kernel,
        grid=(coefs // part,),
        out_shape=(
            jax.ShapeDtypeStruct((coefs, rows), jnp.float32),
            jax.ShapeDtypeStruct((coefs, rows), jnp.float32),
            jax.ShapeDtypeStruct((2, 3), jnp.float32),
        ),
        in_specs=[pl.BlockSpec(sums.shape, lambda i: (0, 0)), block, block, block],
        out_specs=(block, block, pl.BlockSpec((2, 3), lambda i: (0, 0))),
        compiler_params=params(),
        name="finish",
    )(sums, x_t, u_t, v_t)


def along_chips(block, moves):
    return lax.ppermute(block, "grp", [(2 * a + c, 2 * b + c) for a, b in moves for c in range(2)])


def other_core(block):
    return lax.ppermute(block, "grp", [(i, i ^ 1) for i in range(lax.axis_size("grp"))])


def exchange(coded):
    chips = lax.axis_size("grp") // 2
    everyone = [[coded]]
    ring = {
        m: along_chips(coded, [((z + m) % chips, z) for z in range(chips)])
        for m in range(1, chips)
        if not (chips == 4 and m == 2)
    }
    for m in range(1, chips):
        if m in ring:
            everyone.append([ring[m]])
        else:
            everyone.append(
                [along_chips(ring[1], [(1, 0), (2, 1)]), along_chips(ring[3], [(1, 2), (2, 3)])]
            )
    groups, blocks = [], []
    for members in everyone:
        groups += [len(members)] * 2
        blocks += members + [other_core(block) for block in members]
    return tuple(groups), blocks


def far_field(coded, wave_out, wave_in_t, angle, trans_rows):
    blocks = lax.axis_size("blk")
    own = gather_wave(coded, wave_out, angle)
    here = lax.axis_index("blk")
    incoming = jnp.zeros_like(own)
    for turn in range(1, blocks):
        moved = lax.ppermute(own, "blk", [((i - turn) % blocks, i) for i in range(blocks)])
        weights = lax.dynamic_slice_in_dim(trans_rows, (here - turn) % blocks, 1, 0)
        incoming = incoming + weights * moved
    return spread_wave(incoming, wave_in_t, angle)


def body(
    incident,
    mie_coef,
    owner_dev,
    near_row,
    table_id,
    tables,
    wave_out,
    wave_in,
    plane_angle,
    far_trans,
):
    x = incident[0]
    mie = mie_coef[0]
    angle = plane_angle[0]
    rows, coefs = x.shape
    width = -(-coefs // LANES) * LANES
    chips = lax.axis_size("grp") // 2
    devices = lax.axis_size("grp") * lax.axis_size("blk")
    me = lax.axis_index("grp")
    owner = owner_dev[0, :, 0]
    away = ((owner // 2 - me // 2) % chips) * 2 + ((owner % 2) ^ (me % 2))
    slots = 2 * (away * rows + near_row[0])
    table_ids = table_id[0].reshape(rows, -1)
    wave_in_t = wave_in.T

    x_t = x.T
    coded = code(x_t, width)
    groups, shards = exchange(coded)
    far = far_field(coded, wave_out, wave_in_t, angle, far_trans[0, 0])
    image, coded, sums = near_field(groups, slots, table_ids, tables, x, mie, far, shards)

    groups, shards = exchange(coded)
    far = far_field(coded, wave_out, wave_in_t, angle, far_trans[0, 0])
    second_t, _, sums = near_field(
        groups, slots, table_ids, tables, image, mie, far, shards, (x, sums), devices
    )
    sums = lax.all_to_all(sums, ("blk", "grp"), 0, 0, tiled=True)
    solution_t, residual_t, hess_t = finish(sums, x_t, image.T, second_t)
    return solution_t.T[None], residual_t.T[None], hess_t.T


def solution(mesh):
    return jax.shard_map(
        body,
        mesh=mesh,
        in_specs=(
            P("blk", "grp", None),
            P("blk", "grp", None),
            P("blk", "grp", None),
            P("blk", "grp"),
            P("blk", "grp"),
            P(),
            P(),
            P(),
            P("blk", "grp", None),
            P("blk", "grp", None, None),
        ),
        out_specs=(P("blk", "grp", None), P("blk", "grp", None), P()),
        check_vma=False,
    )
```

```python
import functools

import jax
import jax.numpy as jnp
import numpy as np
from jax import lax
from jax.experimental import pallas as pl
from jax.experimental.pallas import tpu as pltpu
from jax.sharding import PartitionSpec as P

epsilon = 1e-06
LANES = 128
CHUNK = 256
BATCH = 32
VMEM_LIMIT = 40 * 2**20


def cosine_coefficients():
    top = 3.1416**2
    nodes = (np.cos((np.arange(400) + 0.5) * np.pi / 400) + 1.0) * top / 2.0
    fit = np.polynomial.chebyshev.Chebyshev.fit(nodes, np.cos(np.sqrt(nodes)), 8, domain=[0.0, top])
    return [float(c) for c in fit.convert(kind=np.polynomial.Polynomial).coef]


COS = cosine_coefficients()


def cosine(angle):
    square = angle * angle
    value = jnp.full_like(square, COS[-1])
    for coef in COS[-2::-1]:
        value = value * square + coef
    return value


def whole(memory=pltpu.VMEM):
    return pl.BlockSpec(memory_space=memory)


def params():
    return pltpu.CompilerParams(vmem_limit_bytes=VMEM_LIMIT)


def pad_lanes(value, width):
    rows, cols = value.shape
    return jnp.concatenate([value, jnp.zeros((rows, width - cols), value.dtype)], axis=1)


def code_kernel(field_ref, coded_ref):
    coefs, rows = field_ref.shape
    width = coded_ref.shape[1]
    for start in range(0, rows, CHUNK):
        part = field_ref[:, pl.ds(start, CHUNK)]
        part = jnp.concatenate([part, jnp.zeros((width - coefs, CHUNK), part.dtype)], axis=0)
        coded_ref[pl.ds(start, CHUNK), :] = part.T.astype(jnp.bfloat16)


def code(field_t, width):
    rows = field_t.shape[1]
    return pl.pallas_call(
        code_kernel,
        out_shape=jax.ShapeDtypeStruct((rows, width), jnp.bfloat16),
        in_specs=[whole()],
        out_specs=whole(),
        compiler_params=params(),
        name="code_rows",
    )(field_t)


def wave_kernel(coded_ref, out_ref, angle_ref, sum_ref):
    coefs, samples = out_ref.shape
    rows = coded_ref.shape[0]

    def part(index, total):
        at = pl.ds(pl.multiple_of(index * CHUNK, CHUNK), CHUNK)
        outgoing = jnp.dot(
            coded_ref[at, :][:, :coefs], out_ref[...], preferred_element_type=jnp.float32
        )
        weighted = cosine(angle_ref[at, :].astype(jnp.float32)) * outgoing
        return total + jnp.sum(weighted, axis=0, keepdims=True)

    sum_ref[...] = lax.fori_loop(0, rows // CHUNK, part, jnp.zeros((1, samples), jnp.float32))


def gather_wave(coded, wave_out, angle):
    rows, samples = angle.shape
    return pl.pallas_call(
        wave_kernel,
        out_shape=jax.ShapeDtypeStruct((1, samples), jnp.float32),
        in_specs=[whole()] * 3,
        out_specs=whole(),
        compiler_params=params(),
        cost_estimate=pl.CostEstimate(
            flops=2 * rows * samples * 256, bytes_accessed=2 * 2**20, transcendentals=0
        ),
        name="gather_wave",
    )(coded, wave_out, angle)


def spread_kernel(incoming_ref, in_ref, angle_ref, far_ref):
    rows = angle_ref.shape[0]

    def part(index, carry):
        at = pl.ds(pl.multiple_of(index * CHUNK, CHUNK), CHUNK)
        spread = cosine(angle_ref[at, :].astype(jnp.float32)) * incoming_ref[...]
        far_ref[at, :] = lax.dot_general(
            spread.astype(jnp.bfloat16),
            in_ref[...],
            (((1,), (1,)), ((), ())),
            preferred_element_type=jnp.float32,
        )
        return carry

    lax.fori_loop(0, rows // CHUNK, part, 0)


def spread_wave(incoming, wave_in_t, angle):
    rows, samples = angle.shape
    coefs = wave_in_t.shape[0]
    return pl.pallas_call(
        spread_kernel,
        out_shape=jax.ShapeDtypeStruct((rows, coefs), jnp.float32),
        in_specs=[whole()] * 3,
        out_specs=whole(),
        compiler_params=params(),
        cost_estimate=pl.CostEstimate(
            flops=2 * rows * samples * 256, bytes_accessed=3 * 2**20, transcendentals=0
        ),
        name="spread_wave",
    )(incoming, wave_in_t, angle)


def near_kernel(groups, second, slot_ref, table_ref, tables_ref, vec_ref, mie_ref, far_ref, *rest):
    if second:
        first_ref, sums_in_ref, *rest = rest
    count = sum(groups)
    shards, (image_ref, other_ref, sums_ref, source, picked) = rest[:count], rest[count:]
    rows, coefs = vec_ref.shape
    requests = slot_ref.shape[0]
    per_row = requests // rows
    width = 2 * LANES
    first = 0
    for place, members in enumerate(groups):
        value = shards[first][...].astype(jnp.float32)
        for member in range(1, members):
            value = value + shards[first + member][...].astype(jnp.float32)
        first += members
        base = place * 2 * rows
        source[pl.ds(base, rows, stride=2), :] = value[:, :LANES]
        source[pl.ds(base + 1, rows, stride=2), :] = value[:, LANES:]

    def pick(step, carry):
        start = pl.multiple_of(step * BATCH, BATCH)
        got = [
            source[pl.ds(pl.multiple_of(slot_ref[start + k], 2), 2), :] for k in range(BATCH)
        ]
        for k in range(0, BATCH, 4):
            picked[pl.ds(pl.multiple_of(2 * (start + k), 8), 8), :] = jnp.concatenate(
                got[k : k + 4], axis=0
            )
        return carry

    lax.fori_loop(0, requests // BATCH, pick, 0)

    def part(index, sums):
        start = pl.multiple_of(index * CHUNK, CHUNK)
        at = pl.ds(start, CHUNK)
        stride = 2 * per_row
        halves = [
            [
                picked[pl.ds(start * stride + 2 * k + h, CHUNK, stride=stride), :].astype(
                    jnp.bfloat16
                )
                for h in range(2)
            ]
            for k in range(per_row)
        ]
        named = [
            jnp.broadcast_to(table_ref[at, k : k + 1], (CHUNK, LANES)).astype(jnp.bfloat16)
            for k in range(per_row)
        ]
        zero = jnp.zeros((CHUNK, LANES), jnp.bfloat16)
        near = jnp.zeros((CHUNK, coefs), jnp.float32)
        for t in range(tables_ref.shape[0]):
            chosen = [named[k] == jnp.bfloat16(t) for k in range(per_row)]
            mixed = []
            for h in range(2):
                value = jnp.where(chosen[0], halves[0][h], zero)
                for k in range(1, per_row):
                    value = value + jnp.where(chosen[k], halves[k][h], zero)
                mixed.append(value)
            near = near + jnp.dot(
                jnp.concatenate(mixed, axis=1)[:, :coefs],
                tables_ref[t],
                preferred_element_type=jnp.float32,
            )
        vec = vec_ref[at, :]
        image = vec - mie_ref[at, :] * (near + far_ref[at, :])

        def dot(a, b):
            return jnp.sum(a * b, axis=0, keepdims=True)

        if second:
            image_ref[:, at] = pad_lanes(image, width).T[:coefs, :]
            new = [dot(first_ref[at, :], image), dot(vec, image), dot(image, image)]
        else:
            image_ref[at, :] = image
            other_ref[at, :] = pad_lanes(image, width).astype(jnp.bfloat16)
            new = [dot(vec, vec), dot(vec, image), dot(image, image)]
        return tuple(a + b for a, b in zip(sums, new, strict=True))

    sums = lax.fori_loop(
        0, rows // CHUNK, part, tuple(jnp.zeros((1, coefs), jnp.float32) for _ in range(3))
    )
    lane = lax.broadcasted_iota(jnp.int32, (1, LANES), 1)
    packed = sums_in_ref[...] if second else jnp.zeros((1, LANES), jnp.float32)
    for k, value in enumerate(sums):
        total = jnp.sum(value, axis=1, keepdims=True)
        packed = jnp.where(lane == k + (3 if second else 0), total, packed)
    sums_ref[...] = jnp.broadcast_to(packed, sums_ref.shape)


def near_field(groups, slots, table_ids, tables, vec, mie, far, shards, second=None, devices=1):
    rows, coefs = vec.shape
    requests = slots.shape[0]
    width = 2 * LANES
    extra = () if second is None else second
    if second is None:
        outs = (
            jax.ShapeDtypeStruct((rows, coefs), jnp.float32),
            jax.ShapeDtypeStruct((rows, width), jnp.bfloat16),
            jax.ShapeDtypeStruct((1, LANES), jnp.float32),
        )
    else:
        outs = (
            jax.ShapeDtypeStruct((coefs, rows), jnp.float32),
            jax.ShapeDtypeStruct((8, LANES), jnp.float32),
            jax.ShapeDtypeStruct((devices, LANES), jnp.float32),
        )
    return pl.pallas_call(
        functools.partial(near_kernel, groups, second is not None),
        out_shape=outs,
        in_specs=[whole(pltpu.SMEM)] + [whole()] * (5 + len(extra) + len(shards)),
        out_specs=(whole(),) * 3,
        scratch_shapes=[
            pltpu.VMEM((len(groups) * rows * 2, LANES), jnp.float32),
            pltpu.VMEM((requests * 2, LANES), jnp.float32),
        ],
        compiler_params=params(),
        cost_estimate=pl.CostEstimate(
            flops=2 * rows * 8 * 256 * 256, bytes_accessed=10 * 2**20, transcendentals=0
        ),
        name="near_second" if second is not None else "near_first",
    )(slots, table_ids, tables, vec, mie, far, *extra, *shards)


def finish_kernel(sums_ref, x_ref, u_ref, v_ref, solution_ref, residual_ref, hess_ref):
    sums = jnp.sum(sums_ref[...], axis=0, keepdims=True)
    xx, xu, uu, xv, uv, vv = [sums[:, k : k + 1] for k in range(6)]
    norm = jnp.sqrt(xx + epsilon)
    inverse = 1.0 / norm
    squared = inverse * inverse
    h11 = xu * squared
    ones = xx * squared
    size1 = uu * squared - 2.0 * h11 * h11 + h11 * h11 * ones
    h21 = jnp.sqrt(jnp.maximum(size1, 0.0) + epsilon)
    q = inverse / h21
    h12 = q * inverse * (xv - h11 * xu)
    h22 = q * q * (uv - h11 * uu - h11 * xv + h11 * h11 * xu)
    size2 = q * q * (vv - 2.0 * h11 * uv + h11 * h11 * uu)
    cross = q * inverse * (xu - h11 * xx)
    twos = size1 / (h21 * h21)
    left = (
        size2
        - 2.0 * h12 * h12
        - 2.0 * h22 * h22
        + h12 * h12 * ones
        + h22 * h22 * twos
        + 2.0 * h12 * h22 * cross
    )
    h32 = jnp.sqrt(jnp.maximum(left, 0.0) + epsilon)
    gram00 = h11 * h11 + h21 * h21
    gram01 = h11 * h12 + h21 * h22
    gram11 = h12 * h12 + h22 * h22 + h32 * h32
    rhs0, rhs1 = norm * h11, norm * h12
    det = gram00 * gram11 - gram01 * gram01
    y1 = (gram11 * rhs0 - gram01 * rhs1) / det
    y2 = (gram00 * rhs1 - gram01 * rhs0) / det
    x, u, v = x_ref[...], u_ref[...], v_ref[...]
    a1, a2 = y1 * inverse, y2 * q
    solution_ref[...] = (a1 - h11 * a2) * x + a2 * u
    residual_ref[...] = x - (a1 - h11 * a2) * u - a2 * v
    hess_ref[0:1, 0:1] = h11
    hess_ref[0:1, 1:2] = h21
    hess_ref[0:1, 2:3] = jnp.zeros_like(h11)
    hess_ref[1:2, 0:1] = h12
    hess_ref[1:2, 1:2] = h22
    hess_ref[1:2, 2:3] = h32


def finish(sums, x_t, u_t, v_t):
    field = jax.ShapeDtypeStruct(x_t.shape, jnp.float32)
    return pl.pallas_call(
        finish_kernel,
        out_shape=(field, field, jax.ShapeDtypeStruct((2, 3), jnp.float32)),
        in_specs=[whole()] * 4,
        out_specs=(whole(),) * 3,
        compiler_params=params(),
        name="finish",
    )(sums, x_t, u_t, v_t)


def along_chips(block, moves):
    return lax.ppermute(block, "grp", [(2 * a + c, 2 * b + c) for a, b in moves for c in range(2)])


def other_core(block, chips):
    return lax.ppermute(block, "grp", [(2 * z + c, 2 * z + 1 - c) for z in chips for c in range(2)])


def line_of_four(coded):
    ends, middle = (0, 3), (1, 2)
    swapped = along_chips(coded, [(0, 1), (1, 0), (2, 3), (3, 2)])
    inner = along_chips(coded, [(1, 2), (2, 1)])
    inward = along_chips(swapped, [(1, 2), (2, 1)])
    outward = along_chips(inner, [(1, 0), (2, 3)])
    last = along_chips(inward, [(1, 0), (2, 3)])
    groups, blocks = [], []
    for members in (
        [(coded, ends + middle)],
        [(swapped, ends + middle)],
        [(inner, middle), (outward, ends)],
        [(inward, middle), (last, ends)],
    ):
        groups += [len(members)] * 2
        blocks += [block for block, _ in members]
        blocks += [other_core(block, chips) for block, chips in members]
    return tuple(groups), blocks


def place_in_line(source, here):
    far_side = 2 + jnp.where((source == 0) | (source == 3), 1, 0)
    return jnp.where(source == here, 0, jnp.where(source == (here ^ 1), 1, far_side))


def ring_of_chips(coded):
    chips = lax.axis_size("grp") // 2
    groups, blocks = [], []
    for m in range(chips):
        block = along_chips(coded, [((z + m) % chips, z) for z in range(chips)]) if m else coded
        groups += [1, 1]
        blocks += [block, other_core(block, range(chips))]
    return tuple(groups), blocks


def exchange(coded):
    return line_of_four(coded) if lax.axis_size("grp") == 8 else ring_of_chips(coded)


def place_of(source, here):
    chips = lax.axis_size("grp") // 2
    return place_in_line(source, here) if chips == 4 else (source - here) % chips


def far_field(coded, wave_out, wave_in_t, angle, trans_rows):
    blocks = lax.axis_size("blk")
    own = gather_wave(coded, wave_out, angle)
    here = lax.axis_index("blk")
    incoming = jnp.zeros_like(own)
    for turn in range(1, blocks):
        moved = lax.ppermute(own, "blk", [((i - turn) % blocks, i) for i in range(blocks)])
        weights = lax.dynamic_slice_in_dim(trans_rows, (here - turn) % blocks, 1, 0)
        incoming = incoming + weights * moved
    return spread_wave(incoming, wave_in_t, angle)


def body(
    incident,
    mie_coef,
    owner_dev,
    near_row,
    table_id,
    tables,
    wave_out,
    wave_in,
    plane_angle,
    far_trans,
):
    x = incident[0]
    mie = mie_coef[0]
    angle = plane_angle[0]
    rows, coefs = x.shape
    width = -(-coefs // LANES) * LANES
    devices = lax.axis_size("grp") * lax.axis_size("blk")
    me = lax.axis_index("grp")
    owner = owner_dev[0, :, 0]
    away = place_of(owner // 2, me // 2) * 2 + ((owner % 2) ^ (me % 2))
    slots = 2 * (away * rows + near_row[0])
    table_ids = table_id[0].reshape(rows, -1)
    wave_in_t = wave_in.T

    x_t = x.T
    coded = code(x_t, width)
    groups, shards = exchange(coded)
    far = far_field(coded, wave_out, wave_in_t, angle, far_trans[0, 0])
    image, coded, sums = near_field(groups, slots, table_ids, tables, x, mie, far, shards)

    groups, shards = exchange(coded)
    far = far_field(coded, wave_out, wave_in_t, angle, far_trans[0, 0])
    second_t, _, sums = near_field(
        groups, slots, table_ids, tables, image, mie, far, shards, (x, sums), devices
    )
    sums = lax.all_to_all(sums, ("blk", "grp"), 0, 0, tiled=True)
    solution_t, residual_t, hess_t = finish(sums, x_t, image.T, second_t)
    return solution_t.T[None], residual_t.T[None], hess_t.T


def solution(mesh):
    return jax.shard_map(
        body,
        mesh=mesh,
        in_specs=(
            P("blk", "grp", None),
            P("blk", "grp", None),
            P("blk", "grp", None),
            P("blk", "grp"),
            P("blk", "grp"),
            P(),
            P(),
            P(),
            P("blk", "grp", None),
            P("blk", "grp", None, None),
        ),
        out_specs=(P("blk", "grp", None), P("blk", "grp", None), P()),
        check_vma=False,
    )
```

```python
import functools

import jax
import jax.numpy as jnp
import numpy as np
from jax import lax
from jax.experimental import pallas as pl
from jax.experimental.pallas import tpu as pltpu
from jax.sharding import PartitionSpec as P

epsilon = 1e-06
LANES = 128
QUAD = 4
CHUNK = 256
BATCH = 32
VMEM_LIMIT = 40 * 2**20


def cosine_coefficients():
    top = 3.1416**2
    nodes = (np.cos((np.arange(400) + 0.5) * np.pi / 400) + 1.0) * top / 2.0
    fit = np.polynomial.chebyshev.Chebyshev.fit(nodes, np.cos(np.sqrt(nodes)), 8, domain=[0.0, top])
    return [float(c) for c in fit.convert(kind=np.polynomial.Polynomial).coef]


COS = cosine_coefficients()


def cosine(angle):
    square = angle * angle
    value = jnp.full_like(square, COS[-1])
    for coef in COS[-2::-1]:
        value = value * square + coef
    return value


def whole(memory=pltpu.VMEM):
    return pl.BlockSpec(memory_space=memory)


def params():
    return pltpu.CompilerParams(vmem_limit_bytes=VMEM_LIMIT)


def pad_lanes(value, width):
    rows, cols = value.shape
    return jnp.concatenate([value, jnp.zeros((rows, width - cols), value.dtype)], axis=1)


def code_kernel(field_ref, coded_ref):
    coefs, rows = field_ref.shape
    width = coded_ref.shape[1]
    for start in range(0, rows, CHUNK):
        part = field_ref[:, pl.ds(start, CHUNK)]
        part = jnp.concatenate([part, jnp.zeros((width - coefs, CHUNK), part.dtype)], axis=0)
        coded_ref[pl.ds(start, CHUNK), :] = part.T.astype(jnp.bfloat16)


def code(field_t, width):
    rows = field_t.shape[1]
    return pl.pallas_call(
        code_kernel,
        out_shape=jax.ShapeDtypeStruct((rows, width), jnp.bfloat16),
        in_specs=[whole()],
        out_specs=whole(),
        compiler_params=params(),
        name="code_rows",
    )(field_t)


def wave_kernel(coded_ref, out_ref, angle_ref, sum_ref):
    coefs, samples = out_ref.shape
    rows = coded_ref.shape[0]

    def part(index, total):
        at = pl.ds(pl.multiple_of(index * CHUNK, CHUNK), CHUNK)
        outgoing = jnp.dot(
            coded_ref[at, :][:, :coefs], out_ref[...], preferred_element_type=jnp.float32
        )
        weighted = cosine(angle_ref[at, :].astype(jnp.float32)) * outgoing
        return total + jnp.sum(weighted, axis=0, keepdims=True)

    sum_ref[...] = lax.fori_loop(0, rows // CHUNK, part, jnp.zeros((1, samples), jnp.float32))


def gather_wave(coded, wave_out, angle):
    rows, samples = angle.shape
    return pl.pallas_call(
        wave_kernel,
        out_shape=jax.ShapeDtypeStruct((1, samples), jnp.float32),
        in_specs=[whole()] * 3,
        out_specs=whole(),
        compiler_params=params(),
        cost_estimate=pl.CostEstimate(
            flops=2 * rows * samples * 256, bytes_accessed=2 * 2**20, transcendentals=0
        ),
        name="gather_wave",
    )(coded, wave_out, angle)


def spread_kernel(incoming_ref, in_ref, angle_ref, far_ref):
    rows = angle_ref.shape[0]

    def part(index, carry):
        at = pl.ds(pl.multiple_of(index * CHUNK, CHUNK), CHUNK)
        spread = cosine(angle_ref[at, :].astype(jnp.float32)) * incoming_ref[...]
        far_ref[at, :] = lax.dot_general(
            spread.astype(jnp.bfloat16),
            in_ref[...],
            (((1,), (1,)), ((), ())),
            preferred_element_type=jnp.float32,
        )
        return carry

    lax.fori_loop(0, rows // CHUNK, part, 0)


def spread_wave(incoming, wave_in_t, angle):
    rows, samples = angle.shape
    coefs = wave_in_t.shape[0]
    return pl.pallas_call(
        spread_kernel,
        out_shape=jax.ShapeDtypeStruct((rows, coefs), jnp.float32),
        in_specs=[whole()] * 3,
        out_specs=whole(),
        compiler_params=params(),
        cost_estimate=pl.CostEstimate(
            flops=2 * rows * samples * 256, bytes_accessed=3 * 2**20, transcendentals=0
        ),
        name="spread_wave",
    )(incoming, wave_in_t, angle)


def load_rows(source, shards):
    rows = shards[0].shape[0]
    for place, shard in enumerate(shards):
        value = shard[...].astype(jnp.float32)
        source[pl.ds(2 * place * rows, rows, stride=2), :] = value[:, :LANES]
        source[pl.ds(2 * place * rows + 1, rows, stride=2), :] = value[:, LANES:]
    source[pl.ds(2 * len(shards) * rows, 8), :] = jnp.zeros((8, LANES), jnp.float32)


def pick_rows(slot_ref, source, picked):
    def pick(step, carry):
        start = pl.multiple_of(step * BATCH, BATCH)
        got = [
            source[pl.ds(pl.multiple_of(slot_ref[start + k], 2), 2), :] for k in range(BATCH)
        ]
        for k in range(0, BATCH, 4):
            picked[pl.ds(pl.multiple_of(2 * (start + k), 8), 8), :] = jnp.concatenate(
                got[k : k + 4], axis=0
            )
        return carry

    lax.fori_loop(0, slot_ref.shape[0] // BATCH, pick, 0)


def translate(start, picked, table_ref, tables_ref):
    at = pl.ds(start, CHUNK)
    per_row = table_ref.shape[1]
    coefs = tables_ref.shape[1]
    stride = 2 * per_row
    halves = [
        [
            picked[pl.ds(start * stride + 2 * k + h, CHUNK, stride=stride), :].astype(jnp.bfloat16)
            for h in range(2)
        ]
        for k in range(per_row)
    ]
    named = [
        jnp.broadcast_to(table_ref[at, k : k + 1], (CHUNK, LANES)).astype(jnp.bfloat16)
        for k in range(per_row)
    ]
    zero = jnp.zeros((CHUNK, LANES), jnp.bfloat16)
    total = jnp.zeros((CHUNK, coefs), jnp.float32)
    for t in range(tables_ref.shape[0]):
        chosen = [named[k] == jnp.bfloat16(t) for k in range(per_row)]
        mixed = []
        for h in range(2):
            value = jnp.where(chosen[0], halves[0][h], zero)
            for k in range(1, per_row):
                value = value + jnp.where(chosen[k], halves[k][h], zero)
            mixed.append(value)
        total = total + jnp.dot(
            jnp.concatenate(mixed, axis=1)[:, :coefs],
            tables_ref[t],
            preferred_element_type=jnp.float32,
        )
    return total


def row_chunks(rows, step, carry=0):
    return lax.fori_loop(
        0, rows // CHUNK, lambda i, c: step(pl.multiple_of(i * CHUNK, CHUNK), c), carry
    )


def serve_kernel(slot_ref, table_ref, tables_ref, *rest):
    *shards, out_ref, source, picked = rest
    load_rows(source, shards)
    pick_rows(slot_ref, source, picked)

    def part(start, carry):
        total = translate(start, picked, table_ref, tables_ref)
        out_ref[pl.ds(start, CHUNK), :] = pad_lanes(total, out_ref.shape[1]).astype(jnp.bfloat16)
        return carry

    row_chunks(out_ref.shape[0], part)


def near_kernel(slot_ref, table_ref, tables_ref, vec_ref, mie_ref, far_ref, *rest):
    *shards, out_ref, source, picked = rest
    load_rows(source, shards)
    pick_rows(slot_ref, source, picked)

    def part(start, carry):
        at = pl.ds(start, CHUNK)
        total = translate(start, picked, table_ref, tables_ref) + far_ref[at, :]
        out_ref[at, :] = vec_ref[at, :] - mie_ref[at, :] * total
        return carry

    row_chunks(out_ref.shape[0], part)


def rows_scratch(shards, requests):
    rows = shards[0].shape[0]
    return [
        pltpu.VMEM((len(shards) * rows * 2 + 8, LANES), jnp.float32),
        pltpu.VMEM((requests * 2, LANES), jnp.float32),
    ]


def product_cost(rows, tables):
    return pl.CostEstimate(
        flops=2 * rows * tables * 256 * 256, bytes_accessed=8 * 2**20, transcendentals=0
    )


def serve(slots, table_ids, tables, shards):
    rows, width = shards[0].shape
    return pl.pallas_call(
        serve_kernel,
        out_shape=jax.ShapeDtypeStruct((rows, width), jnp.bfloat16),
        in_specs=[whole(pltpu.SMEM)] + [whole()] * (2 + len(shards)),
        out_specs=whole(),
        scratch_shapes=rows_scratch(shards, slots.shape[0]),
        compiler_params=params(),
        cost_estimate=product_cost(rows, tables.shape[0]),
        name="serve",
    )(slots, table_ids, tables, *shards)


def near_field(slots, table_ids, tables, vec, mie, far, shards):
    return pl.pallas_call(
        near_kernel,
        out_shape=jax.ShapeDtypeStruct(vec.shape, jnp.float32),
        in_specs=[whole(pltpu.SMEM)] + [whole()] * (5 + len(shards)),
        out_specs=whole(),
        scratch_shapes=rows_scratch(shards, slots.shape[0]),
        compiler_params=params(),
        cost_estimate=product_cost(vec.shape[0], tables.shape[0]),
        name="near_field",
    )(slots, table_ids, tables, vec, mie, far, *shards)


def join_kernel(second, count, base_ref, mie_ref, vec_ref, *rest):
    served, rest = rest[:count], rest[count:]
    if second:
        first_ref, sums_in_ref, *rest = rest
    image_ref, *rest, sums_ref = rest
    rows, coefs = base_ref.shape
    width = served[0].shape[1]

    def dot(a, b):
        return jnp.sum(a * b, axis=0, keepdims=True)

    def part(start, sums):
        at = pl.ds(start, CHUNK)
        far_rows = served[0][at, :].astype(jnp.float32)
        for other in served[1:]:
            far_rows = far_rows + other[at, :].astype(jnp.float32)
        image = base_ref[at, :] - mie_ref[at, :] * far_rows[:, :coefs]
        vec = vec_ref[at, :]
        if second:
            image_ref[:, at] = pad_lanes(image, width).T[:coefs, :]
            new = [dot(first_ref[at, :], image), dot(vec, image), dot(image, image)]
        else:
            image_ref[at, :] = image
            rest[0][at, :] = pad_lanes(image, width).astype(jnp.bfloat16)
            new = [dot(vec, vec), dot(vec, image), dot(image, image)]
        return tuple(a + b for a, b in zip(sums, new, strict=True))

    sums = row_chunks(rows, part, tuple(jnp.zeros((1, coefs), jnp.float32) for _ in range(3)))
    lane = lax.broadcasted_iota(jnp.int32, (1, LANES), 1)
    packed = sums_in_ref[...] if second else jnp.zeros((1, LANES), jnp.float32)
    for k, value in enumerate(sums):
        total = jnp.sum(value, axis=1, keepdims=True)
        packed = jnp.where(lane == k + (3 if second else 0), total, packed)
    sums_ref[...] = jnp.broadcast_to(packed, sums_ref.shape)


def join(base, mie, vec, served, second=None, devices=1):
    rows, coefs = base.shape
    width = served[0].shape[1]
    if second is None:
        second = ()
        outs = (
            jax.ShapeDtypeStruct((rows, coefs), jnp.float32),
            jax.ShapeDtypeStruct((rows, width), jnp.bfloat16),
            jax.ShapeDtypeStruct((1, LANES), jnp.float32),
        )
    else:
        outs = (
            jax.ShapeDtypeStruct((coefs, rows), jnp.float32),
            jax.ShapeDtypeStruct((devices, LANES), jnp.float32),
        )
    return pl.pallas_call(
        functools.partial(join_kernel, len(second) > 0, len(served)),
        out_shape=outs,
        in_specs=[whole()] * (3 + len(served) + len(second)),
        out_specs=(whole(),) * len(outs),
        compiler_params=params(),
        name="join_second" if second else "join_first",
    )(base, mie, vec, *served, *second)


def finish_kernel(sums_ref, x_ref, u_ref, v_ref, solution_ref, residual_ref, hess_ref):
    sums = jnp.sum(sums_ref[...], axis=0, keepdims=True)
    xx, xu, uu, xv, uv, vv = [sums[:, k : k + 1] for k in range(6)]
    norm = jnp.sqrt(xx + epsilon)
    inverse = 1.0 / norm
    squared = inverse * inverse
    h11 = xu * squared
    ones = xx * squared
    size1 = uu * squared - 2.0 * h11 * h11 + h11 * h11 * ones
    h21 = jnp.sqrt(jnp.maximum(size1, 0.0) + epsilon)
    q = inverse / h21
    h12 = q * inverse * (xv - h11 * xu)
    h22 = q * q * (uv - h11 * uu - h11 * xv + h11 * h11 * xu)
    size2 = q * q * (vv - 2.0 * h11 * uv + h11 * h11 * uu)
    cross = q * inverse * (xu - h11 * xx)
    twos = size1 / (h21 * h21)
    left = (
        size2
        - 2.0 * h12 * h12
        - 2.0 * h22 * h22
        + h12 * h12 * ones
        + h22 * h22 * twos
        + 2.0 * h12 * h22 * cross
    )
    h32 = jnp.sqrt(jnp.maximum(left, 0.0) + epsilon)
    gram00 = h11 * h11 + h21 * h21
    gram01 = h11 * h12 + h21 * h22
    gram11 = h12 * h12 + h22 * h22 + h32 * h32
    rhs0, rhs1 = norm * h11, norm * h12
    det = gram00 * gram11 - gram01 * gram01
    y1 = (gram11 * rhs0 - gram01 * rhs1) / det
    y2 = (gram00 * rhs1 - gram01 * rhs0) / det
    x, u, v = x_ref[...], u_ref[...], v_ref[...]
    a1, a2 = y1 * inverse, y2 * q
    solution_ref[...] = (a1 - h11 * a2) * x + a2 * u
    residual_ref[...] = x - (a1 - h11 * a2) * u - a2 * v
    hess_ref[0:1, 0:1] = h11
    hess_ref[0:1, 1:2] = h21
    hess_ref[0:1, 2:3] = jnp.zeros_like(h11)
    hess_ref[1:2, 0:1] = h12
    hess_ref[1:2, 1:2] = h22
    hess_ref[1:2, 2:3] = h32


def finish(sums, x_t, u_t, v_t):
    field = jax.ShapeDtypeStruct(x_t.shape, jnp.float32)
    return pl.pallas_call(
        finish_kernel,
        out_shape=(field, field, jax.ShapeDtypeStruct((2, 3), jnp.float32)),
        in_specs=[whole()] * 4,
        out_specs=(whole(),) * 3,
        compiler_params=params(),
        name="finish",
    )(sums, x_t, u_t, v_t)


def flip(block, bits):
    return lax.ppermute(block, "grp", [(i, i ^ bits) for i in range(lax.axis_size("grp"))])


def far_field(coded, wave_out, wave_in_t, angle, trans_rows):
    blocks = lax.axis_size("blk")
    own = gather_wave(coded, wave_out, angle)
    here = lax.axis_index("blk")
    incoming = jnp.zeros_like(own)
    for turn in range(1, blocks):
        moved = lax.ppermute(own, "blk", [((i - turn) % blocks, i) for i in range(blocks)])
        weights = lax.dynamic_slice_in_dim(trans_rows, (here - turn) % blocks, 1, 0)
        incoming = incoming + weights * moved
    return spread_wave(incoming, wave_in_t, angle)


def body(
    incident,
    mie_coef,
    owner_dev,
    near_row,
    table_id,
    tables,
    wave_out,
    wave_in,
    plane_angle,
    far_trans,
):
    x = incident[0]
    mie = mie_coef[0]
    angle = plane_angle[0]
    rows, coefs = x.shape
    width = -(-coefs // LANES) * LANES
    group = lax.axis_size("grp")
    devices = group * lax.axis_size("blk")
    tables_count = tables.shape[0]
    wave_in_t = wave_in.T
    x_t = x.T

    apart = owner_dev[0, :, 0] ^ lax.axis_index("grp")
    slots = 2 * ((apart % QUAD) * rows + near_row[0])
    nothing = 2 * QUAD * rows
    names = table_id[0]
    quads = range(1, group // QUAD)
    asked = [
        flip(jnp.where(apart // QUAD == j, slots, nothing) * tables_count + names, QUAD * j)
        for j in quads
    ]
    asked = [(word // tables_count, (word % tables_count).reshape(rows, -1)) for word in asked]
    slots = jnp.where(apart < QUAD, slots, nothing)
    names = names.reshape(rows, -1)

    def operator(coded, vec):
        across = flip(coded, 2)
        shards = [coded, flip(coded, 1), across, flip(across, 1)]
        far = far_field(coded, wave_out, wave_in_t, angle, far_trans[0, 0])
        served = [
            flip(serve(slot, name, tables, shards), QUAD * j)
            for j, (slot, name) in zip(quads, asked, strict=True)
        ]
        return near_field(slots, names, tables, vec, mie, far, shards), served

    base, served = operator(code(x_t, width), x)
    image, coded, sums = join(base, mie, x, served)
    base, served = operator(coded, image)
    second_t, sums = join(base, mie, image, served, (x, sums), devices)
    sums = lax.all_to_all(sums, ("blk", "grp"), 0, 0, tiled=True)
    solution_t, residual_t, hess_t = finish(sums, x_t, image.T, second_t)
    return solution_t.T[None], residual_t.T[None], hess_t.T


def solution(mesh):
    return jax.shard_map(
        body,
        mesh=mesh,
        in_specs=(
            P("blk", "grp", None),
            P("blk", "grp", None),
            P("blk", "grp", None),
            P("blk", "grp"),
            P("blk", "grp"),
            P(),
            P(),
            P(),
            P("blk", "grp", None),
            P("blk", "grp", None, None),
        ),
        out_specs=(P("blk", "grp", None), P("blk", "grp", None), P()),
        check_vma=False,
    )
```

```python
import functools

import jax
import jax.numpy as jnp
import numpy as np
from jax import lax
from jax.experimental import pallas as pl
from jax.experimental.pallas import tpu as pltpu
from jax.sharding import PartitionSpec as P

epsilon = 1e-06
LANES = 128
QUAD = 4
CHUNK = 256
BATCH = 32
VMEM_LIMIT = 16 * 2**20
COST = pl.CostEstimate(flops=1, bytes_accessed=1, transcendentals=0)


def cosine_coefficients():
    top = 3.1416**2
    nodes = (np.cos((np.arange(400) + 0.5) * np.pi / 400) + 1.0) * top / 2.0
    fit = np.polynomial.chebyshev.Chebyshev.fit(nodes, np.cos(np.sqrt(nodes)), 8, domain=[0.0, top])
    return [float(c) for c in fit.convert(kind=np.polynomial.Polynomial).coef]


COS = cosine_coefficients()


def cosine(angle):
    square = angle * angle
    value = jnp.full_like(square, COS[-1])
    for coef in COS[-2::-1]:
        value = value * square + coef
    return value


def whole(memory=pltpu.VMEM):
    return pl.BlockSpec(memory_space=memory)


def params():
    return pltpu.CompilerParams(vmem_limit_bytes=VMEM_LIMIT)


def pad_lanes(value, width):
    rows, cols = value.shape
    return jnp.concatenate([value, jnp.zeros((rows, width - cols), value.dtype)], axis=1)


def code_kernel(field_ref, coded_ref):
    coefs, rows = field_ref.shape
    width = coded_ref.shape[1]
    for start in range(0, rows, CHUNK):
        part = field_ref[:, pl.ds(start, CHUNK)]
        part = jnp.concatenate([part, jnp.zeros((width - coefs, CHUNK), part.dtype)], axis=0)
        coded_ref[pl.ds(start, CHUNK), :] = part.T.astype(jnp.bfloat16)


def code(field_t, width):
    rows = field_t.shape[1]
    return pl.pallas_call(
        code_kernel,
        out_shape=jax.ShapeDtypeStruct((rows, width), jnp.bfloat16),
        in_specs=[whole()],
        out_specs=whole(),
        compiler_params=params(),
        name="code_rows",
    )(field_t)


def wave_kernel(coded_ref, out_ref, angle_ref, sum_ref):
    coefs, samples = out_ref.shape
    rows = coded_ref.shape[0]

    def part(index, total):
        at = pl.ds(pl.multiple_of(index * CHUNK, CHUNK), CHUNK)
        outgoing = jnp.dot(
            coded_ref[at, :][:, :coefs], out_ref[...], preferred_element_type=jnp.float32
        )
        weighted = cosine(angle_ref[at, :].astype(jnp.float32)) * outgoing
        return total + jnp.sum(weighted, axis=0, keepdims=True)

    sum_ref[...] = lax.fori_loop(0, rows // CHUNK, part, jnp.zeros((1, samples), jnp.float32))


def gather_wave(coded, wave_out, angle):
    rows, samples = angle.shape
    return pl.pallas_call(
        wave_kernel,
        out_shape=jax.ShapeDtypeStruct((1, samples), jnp.float32),
        in_specs=[whole()] * 3,
        out_specs=whole(),
        compiler_params=params(),
        cost_estimate=COST,
        name="gather_wave",
    )(coded, wave_out, angle)


def spread_kernel(incoming_ref, in_ref, angle_ref, far_ref):
    rows = angle_ref.shape[0]

    def part(index, carry):
        at = pl.ds(pl.multiple_of(index * CHUNK, CHUNK), CHUNK)
        spread = cosine(angle_ref[at, :].astype(jnp.float32)) * incoming_ref[...]
        far_ref[at, :] = lax.dot_general(
            spread.astype(jnp.bfloat16),
            in_ref[...],
            (((1,), (1,)), ((), ())),
            preferred_element_type=jnp.float32,
        )
        return carry

    lax.fori_loop(0, rows // CHUNK, part, 0)


def spread_wave(incoming, wave_in_t, angle):
    rows, samples = angle.shape
    coefs = wave_in_t.shape[0]
    return pl.pallas_call(
        spread_kernel,
        out_shape=jax.ShapeDtypeStruct((rows, coefs), jnp.float32),
        in_specs=[whole()] * 3,
        out_specs=whole(),
        compiler_params=params(),
        cost_estimate=COST,
        name="spread_wave",
    )(incoming, wave_in_t, angle)


def load_rows(source, shards):
    rows = shards[0].shape[0]
    for place, shard in enumerate(shards):
        value = shard[...].astype(jnp.float32)
        source[pl.ds(2 * place * rows, rows, stride=2), :] = value[:, :LANES]
        source[pl.ds(2 * place * rows + 1, rows, stride=2), :] = value[:, LANES:]
    source[pl.ds(2 * len(shards) * rows, 8), :] = jnp.zeros((8, LANES), jnp.float32)


def pick_rows(slot_ref, source, picked):
    def pick(step, carry):
        start = pl.multiple_of(step * BATCH, BATCH)
        got = [
            source[pl.ds(pl.multiple_of(slot_ref[start + k], 2), 2), :] for k in range(BATCH)
        ]
        for k in range(0, BATCH, 4):
            picked[pl.ds(pl.multiple_of(2 * (start + k), 8), 8), :] = jnp.concatenate(
                got[k : k + 4], axis=0
            )
        return carry

    lax.fori_loop(0, slot_ref.shape[0] // BATCH, pick, 0)


def translate(start, picked, table_ref, tables_ref):
    at = pl.ds(start, CHUNK)
    per_row = table_ref.shape[1]
    coefs = tables_ref.shape[1]
    stride = 2 * per_row
    halves = [
        [
            picked[pl.ds(start * stride + 2 * k + h, CHUNK, stride=stride), :].astype(jnp.bfloat16)
            for h in range(2)
        ]
        for k in range(per_row)
    ]
    named = [
        jnp.broadcast_to(table_ref[at, k : k + 1], (CHUNK, LANES)).astype(jnp.bfloat16)
        for k in range(per_row)
    ]
    zero = jnp.zeros((CHUNK, LANES), jnp.bfloat16)
    total = jnp.zeros((CHUNK, coefs), jnp.float32)
    for t in range(tables_ref.shape[0]):
        chosen = [named[k] == jnp.bfloat16(t) for k in range(per_row)]
        mixed = []
        for h in range(2):
            value = jnp.where(chosen[0], halves[0][h], zero)
            for k in range(1, per_row):
                value = value + jnp.where(chosen[k], halves[k][h], zero)
            mixed.append(value)
        total = total + jnp.dot(
            jnp.concatenate(mixed, axis=1)[:, :coefs],
            tables_ref[t],
            preferred_element_type=jnp.float32,
        )
    return total


def row_chunks(rows, step, carry=0):
    return lax.fori_loop(
        0, rows // CHUNK, lambda i, c: step(pl.multiple_of(i * CHUNK, CHUNK), c), carry
    )


def serve_kernel(active_ref, slot_ref, table_ref, tables_ref, *rest):
    *shards, out_ref, source, picked = rest

    def part(start, carry):
        total = translate(start, picked, table_ref, tables_ref)
        out_ref[pl.ds(start, CHUNK), :] = pad_lanes(total, out_ref.shape[1]).astype(jnp.bfloat16)
        return carry

    @pl.when(active_ref[0] != 0)
    def _():
        load_rows(source, shards)
        pick_rows(slot_ref, source, picked)
        row_chunks(out_ref.shape[0], part)


def near_kernel(slot_ref, table_ref, tables_ref, mie_ref, far_ref, *rest):
    *shards, out_ref, source, picked = rest
    load_rows(source, shards)
    pick_rows(slot_ref, source, picked)

    def part(start, carry):
        at = pl.ds(start, CHUNK)
        total = translate(start, picked, table_ref, tables_ref) + far_ref[at, :]
        out_ref[at, :] = mie_ref[at, :] * total
        return carry

    row_chunks(out_ref.shape[0], part)


def rows_scratch(shards, requests):
    rows = shards[0].shape[0]
    return [
        pltpu.VMEM((len(shards) * rows * 2 + 8, LANES), jnp.float32),
        pltpu.VMEM((requests * 2, LANES), jnp.float32),
    ]


def serve(active, slots, table_ids, tables, shards):
    rows, width = shards[0].shape
    return pl.pallas_call(
        serve_kernel,
        out_shape=jax.ShapeDtypeStruct((rows, width), jnp.bfloat16),
        in_specs=[whole(pltpu.SMEM)] * 2 + [whole()] * (2 + len(shards)),
        out_specs=whole(),
        scratch_shapes=rows_scratch(shards, slots.shape[0]),
        compiler_params=params(),
        cost_estimate=COST,
        name="serve",
    )(active.astype(jnp.int32).reshape(1), slots, table_ids, tables, *shards)


def near_field(slots, table_ids, tables, mie, far, shards):
    return pl.pallas_call(
        near_kernel,
        out_shape=jax.ShapeDtypeStruct(mie.shape, jnp.float32),
        in_specs=[whole(pltpu.SMEM)] + [whole()] * (4 + len(shards)),
        out_specs=whole(),
        scratch_shapes=rows_scratch(shards, slots.shape[0]),
        compiler_params=params(),
        cost_estimate=COST,
        name="near_field",
    )(slots, table_ids, tables, mie, far, *shards)


def join_kernel(second, count, base_ref, mie_ref, x_ref, *rest):
    served, rest = rest[:count], rest[count:]
    if second:
        vec_ref, sums_in_ref, *rest = rest
    else:
        vec_ref = x_ref
    image_ref, *rest, sums_ref = rest
    rows, coefs = base_ref.shape
    width = served[0].shape[1]

    def dot(a, b):
        return jnp.sum(a * b, axis=0, keepdims=True)

    def part(start, sums):
        at = pl.ds(start, CHUNK)
        far_rows = served[0][at, :].astype(jnp.float32)
        for other in served[1:]:
            far_rows = far_rows + other[at, :].astype(jnp.float32)
        image = base_ref[at, :] + mie_ref[at, :] * far_rows[:, :coefs]
        wide = pad_lanes(image, width)
        if not second:
            rest[0][at, :] = wide.astype(jnp.bfloat16)
        image = wide.T[:coefs, :]
        image_ref[:, at] = image
        x, vec = x_ref[:, at], vec_ref[:, at]
        new = [dot(x, image), dot(vec, image) if second else dot(x, x), dot(image, image)]
        return tuple(a + b for a, b in zip(sums, new, strict=True))

    sums = row_chunks(rows, part, tuple(jnp.zeros((1, CHUNK), jnp.float32) for _ in range(3)))
    lane = lax.broadcasted_iota(jnp.int32, (1, LANES), 1)
    packed = sums_in_ref[...] if second else jnp.zeros((1, LANES), jnp.float32)
    for k, value in enumerate(sums):
        total = jnp.sum(value, axis=1, keepdims=True)
        packed = jnp.where(lane == k + (3 if second else 0), total, packed)
    sums_ref[...] = jnp.broadcast_to(packed, sums_ref.shape)


def join(base, mie, x_t, served, second=(), devices=1):
    rows, coefs = base.shape
    width = served[0].shape[1]
    outs = [jax.ShapeDtypeStruct((coefs, rows), jnp.float32)]
    if not second:
        outs.append(jax.ShapeDtypeStruct((rows, width), jnp.bfloat16))
    outs.append(jax.ShapeDtypeStruct((devices, LANES), jnp.float32))
    return pl.pallas_call(
        functools.partial(join_kernel, len(second) > 0, len(served)),
        out_shape=tuple(outs),
        in_specs=[whole()] * (3 + len(served) + len(second)),
        out_specs=(whole(),) * len(outs),
        compiler_params=params(),
        name="join_second" if second else "join_first",
    )(base, mie, x_t, *served, *second)


def finish_kernel(sums_ref, x_ref, b_ref, c_ref, solution_ref, residual_ref, hess_ref):
    sums = jnp.sum(sums_ref[...], axis=0, keepdims=True)
    xb, xx, bb, xc, bc, cc = [sums[:, k : k + 1] for k in range(6)]
    norm = jnp.sqrt(xx + epsilon)
    inverse = 1.0 / norm
    squared = inverse * inverse
    h11 = (xx - xb) * squared
    g = (xb + epsilon) * squared
    size1 = (g * g * xx - 2.0 * g * xb + bb) * squared
    h21 = jnp.sqrt(jnp.maximum(size1, 0.0) + epsilon)
    q = inverse / h21
    v11 = xx * squared
    v12 = q * inverse * (g * xx - xb)
    v22 = size1 / (h21 * h21)
    p1 = q * inverse * (g * xb - xc)
    p2 = q * q * (g * g * xb - g * xc - g * bb + bc)
    pp = q * q * (g * g * bb - 2.0 * g * bc + cc)
    h12 = v12 - p1
    h22 = v22 - p2
    rest = 1.0 - h22
    size2 = (
        rest * rest * v22
        + h12 * h12 * v11
        + pp
        - 2.0 * rest * h12 * v12
        - 2.0 * rest * p2
        + 2.0 * h12 * p1
    )
    h32 = jnp.sqrt(jnp.maximum(size2, 0.0) + epsilon)
    gram00 = h11 * h11 + h21 * h21
    gram01 = h11 * h12 + h21 * h22
    gram11 = h12 * h12 + h22 * h22 + h32 * h32
    rhs0, rhs1 = norm * h11, norm * h12
    det = gram00 * gram11 - gram01 * gram01
    a1 = (gram11 * rhs0 - gram01 * rhs1) / det * inverse
    a2 = (gram00 * rhs1 - gram01 * rhs0) / det * q
    x, b, c = x_ref[...], b_ref[...], c_ref[...]
    solution_ref[...] = (a1 + a2 * g) * x - a2 * b
    residual_ref[...] = (1.0 - a1 - a2 * g) * x + (a1 + a2 * (1.0 + g)) * b - a2 * c
    hess_ref[0:1, 0:1] = h11
    hess_ref[0:1, 1:2] = h21
    hess_ref[0:1, 2:3] = jnp.zeros_like(h11)
    hess_ref[1:2, 0:1] = h12
    hess_ref[1:2, 1:2] = h22
    hess_ref[1:2, 2:3] = h32


def finish(sums, x_t, b_t, c_t):
    field = jax.ShapeDtypeStruct(x_t.shape, jnp.float32)
    return pl.pallas_call(
        finish_kernel,
        out_shape=(field, field, jax.ShapeDtypeStruct((2, 3), jnp.float32)),
        in_specs=[whole()] * 4,
        out_specs=(whole(),) * 3,
        compiler_params=params(),
        name="finish",
    )(sums, x_t, b_t, c_t)


def flip(block, bits):
    return lax.ppermute(block, "grp", [(i, i ^ bits) for i in range(lax.axis_size("grp"))])


def along_chips(block, moves):
    return lax.ppermute(block, "grp", [(2 * a + c, 2 * b + c) for a, b in moves for c in range(2)])


def other_core(block, chips):
    return lax.ppermute(block, "grp", [(2 * z + c, 2 * z + 1 - c) for z in chips for c in range(2)])


def once(*values):
    return lax.optimization_barrier(values)


class Quads:
    def __init__(self, apart):
        self.others = range(1, lax.axis_size("grp") // QUAD)
        self.here = jnp.where(apart < QUAD, apart, -1)
        self.asked = [jnp.where(apart // QUAD == j, apart % QUAD, -1) for j in self.others]
        self.places = QUAD

    def ask(self, words):
        return [flip(word, QUAD * j) for j, word in zip(self.others, words, strict=True)]

    def operator(self, coded, work):
        across = flip(coded, 2)
        same = flip(coded, 1)
        waves = work.waves(coded, 1)
        across, waves, work.asked, work.local = once(across, waves, work.asked, work.local)
        shards = [coded, same, across, flip(across, 1)]
        on = jnp.ones((), jnp.bool_)
        served = [flip(work.serve(on, k, shards), QUAD * j) for k, j in enumerate(self.others)]
        return work.near(work.far(waves), shards), served


class Line:
    def __init__(self, apart):
        chip, core = apart // 2, apart % 2
        here = lax.axis_index("grp") // 2
        self.middle = (here == 1) | (here == 2)
        inner = (chip == 3) & self.middle
        self.here = jnp.where(chip < 2, apart, jnp.where(inner, QUAD + core, -1))
        self.places = QUAD + 2

    def operator(self, coded, work):
        across = along_chips(coded, [(0, 1), (1, 0), (2, 3), (3, 2)])
        inner = along_chips(coded, [(1, 2), (2, 1)])
        shards = [coded, flip(coded, 1)]
        sums = work.serve(~self.middle, 0, shards)
        early = along_chips(sums, [(0, 2), (3, 1)])
        waves = work.waves(once(coded, sums)[0], 2)
        across, inner, waves = once(across, inner, waves)
        shards = shards + [across, flip(across, 1)]
        sums = work.serve(self.middle, 0, shards)
        late = along_chips(sums, [(1, 3), (2, 0)])
        inner = once(inner, sums)[0]
        far, early = once(work.far(waves), early)
        return work.near(far, shards + [inner, other_core(inner, (1, 2))]), [early, late]


def wave_swaps(waves, count):
    blocks = lax.axis_size("blk")
    while waves.shape[0] < min(count, blocks):
        bits = waves.shape[0]
        moved = lax.ppermute(waves, "blk", [(i, i ^ bits) for i in range(blocks)])
        waves = jnp.concatenate([waves, moved], axis=0)
    return waves


def body(
    incident,
    mie_coef,
    owner_dev,
    near_row,
    table_id,
    tables,
    wave_out,
    wave_in,
    plane_angle,
    far_trans,
):
    x = incident[0]
    mie = mie_coef[0]
    angle = plane_angle[0]
    rows, coefs = x.shape
    width = -(-coefs // LANES) * LANES
    group = lax.axis_size("grp")
    devices = group * lax.axis_size("blk")
    tables_count = tables.shape[0]
    wave_in_t = wave_in.T
    x_t = x.T

    apart = owner_dev[0, :, 0] ^ lax.axis_index("grp")
    first = Quads(apart)
    second = Line(apart) if group == 2 * QUAD else first
    names = table_id[0]

    def slots_of(place, places):
        return 2 * jnp.where(place < 0, places * rows, place * rows + near_row[0])

    words = first.ask([slots_of(place, QUAD) * tables_count + names for place in first.asked])
    blocks = lax.axis_size("blk")
    turns = jnp.arange(blocks, dtype=jnp.int32)
    weights = far_trans[0, 0][turns ^ lax.axis_index("blk")]
    weights = jnp.where(turns[:, None] > 0, weights, 0.0)

    class Work:
        asked = [(word // tables_count, (word % tables_count).reshape(rows, -1)) for word in words]
        local = (names.reshape(rows, -1), mie)

        def __init__(self, form):
            self.slots = slots_of(form.here, form.places)

        def serve(self, active, which, shards):
            slot, name = self.asked[which]
            slot = jnp.minimum(slot, 2 * len(shards) * rows)
            return serve(active, slot, name, tables, shards)

        def waves(self, coded, count):
            return wave_swaps(gather_wave(coded, wave_out, angle), count)

        def far(self, waves):
            waves = wave_swaps(waves, blocks)
            incoming = jnp.sum(weights * waves, axis=0, keepdims=True)
            return spread_wave(incoming, wave_in_t, angle)

        def near(self, far, shards):
            names, mie = self.local
            return near_field(self.slots, names, tables, mie, far, shards)

    work = Work(first)
    base, served = first.operator(code(x_t, width), work)
    names, mie = work.local
    b_t, coded, sums = join(base, mie, x_t, served)
    again = Work(second)
    again.asked, again.local = work.asked, work.local
    base, served = second.operator(coded, again)
    c_t, sums = join(base, mie, x_t, served, (b_t, sums), devices)
    sums = lax.all_to_all(sums, ("blk", "grp"), 0, 0, tiled=True)
    solution_t, residual_t, hess_t = finish(sums, x_t, b_t, c_t)
    return solution_t.T[None], residual_t.T[None], hess_t.T


def solution(mesh):
    return jax.shard_map(
        body,
        mesh=mesh,
        in_specs=(
            P("blk", "grp", None),
            P("blk", "grp", None),
            P("blk", "grp", None),
            P("blk", "grp"),
            P("blk", "grp"),
            P(),
            P(),
            P(),
            P("blk", "grp", None),
            P("blk", "grp", None, None),
        ),
        out_specs=(P("blk", "grp", None), P("blk", "grp", None), P()),
        check_vma=False,
    )
```

```python
import functools

import jax
import jax.numpy as jnp
import numpy as np
from jax import lax
from jax.experimental import pallas as pl
from jax.experimental.pallas import tpu as pltpu
from jax.sharding import PartitionSpec as P

epsilon = 1e-06
LANES = 128
QUAD = 4
CHUNK = 512
BATCH = 32
VMEM_LIMIT = 16 * 2**20
COST = pl.CostEstimate(flops=1, bytes_accessed=1, transcendentals=0)


def cosine_coefficients():
    top = 3.1416**2
    nodes = (np.cos((np.arange(400) + 0.5) * np.pi / 400) + 1.0) * top / 2.0
    fit = np.polynomial.chebyshev.Chebyshev.fit(nodes, np.cos(np.sqrt(nodes)), 8, domain=[0.0, top])
    return [float(c) for c in fit.convert(kind=np.polynomial.Polynomial).coef]


COS = cosine_coefficients()


def cosine(angle):
    square = angle * angle
    value = jnp.full_like(square, COS[-1])
    for coef in COS[-2::-1]:
        value = value * square + coef
    return value


def whole(memory=pltpu.VMEM):
    return pl.BlockSpec(memory_space=memory)


def params():
    return pltpu.CompilerParams(vmem_limit_bytes=VMEM_LIMIT)


def pad_lanes(value, width):
    rows, cols = value.shape
    return jnp.concatenate([value, jnp.zeros((rows, width - cols), value.dtype)], axis=1)


def code_kernel(field_ref, coded_ref):
    coefs, rows = field_ref.shape
    width = coded_ref.shape[1]
    for start in range(0, rows, CHUNK):
        part = field_ref[:, pl.ds(start, CHUNK)]
        part = jnp.concatenate([part, jnp.zeros((width - coefs, CHUNK), part.dtype)], axis=0)
        coded_ref[pl.ds(start, CHUNK), :] = part.T.astype(jnp.bfloat16)


def code(field_t, width):
    rows = field_t.shape[1]
    return pl.pallas_call(
        code_kernel,
        out_shape=jax.ShapeDtypeStruct((rows, width), jnp.bfloat16),
        in_specs=[whole()],
        out_specs=whole(),
        compiler_params=params(),
        name="code_rows",
    )(field_t)


def wave_kernel(coded_ref, out_ref, angle_ref, sum_ref):
    coefs, samples = out_ref.shape
    rows = coded_ref.shape[0]

    def part(index, total):
        at = pl.ds(pl.multiple_of(index * CHUNK, CHUNK), CHUNK)
        outgoing = jnp.dot(
            coded_ref[at, :][:, :coefs], out_ref[...], preferred_element_type=jnp.float32
        )
        weighted = cosine(angle_ref[at, :].astype(jnp.float32)) * outgoing
        return total + jnp.sum(weighted, axis=0, keepdims=True)

    sum_ref[...] = lax.fori_loop(0, rows // CHUNK, part, jnp.zeros((1, samples), jnp.float32))


def gather_wave(coded, wave_out, angle):
    rows, samples = angle.shape
    return pl.pallas_call(
        wave_kernel,
        out_shape=jax.ShapeDtypeStruct((1, samples), jnp.float32),
        in_specs=[whole()] * 3,
        out_specs=whole(),
        compiler_params=params(),
        cost_estimate=COST,
        name="gather_wave",
    )(coded, wave_out, angle)


def spread_wave(at, incoming_ref, in_ref, angle_ref):
    spread = cosine(angle_ref[at, :].astype(jnp.float32)) * incoming_ref[...]
    return lax.dot_general(
        spread.astype(jnp.bfloat16),
        in_ref[...],
        (((1,), (1,)), ((), ())),
        preferred_element_type=jnp.float32,
    )


def load_rows(source, first, shards):
    rows = shards[0].shape[0]
    for place, shard in enumerate(shards, first):
        value = shard[...].astype(jnp.float32)
        source[pl.ds(2 * place * rows, rows, stride=2), :] = value[:, :LANES]
        source[pl.ds(2 * place * rows + 1, rows, stride=2), :] = value[:, LANES:]


def pick_rows(source_ref, target_ref, bound_ref, segments, source, picked):
    picked[...] = jnp.zeros_like(picked)

    def move(places, shift):
        got = [source[pl.ds(pl.multiple_of(source_ref[n] + shift, 2), 2), :] for n in places]
        for n, row in zip(places, got, strict=True):
            picked[pl.ds(pl.multiple_of(target_ref[n], 2), 2), :] = row

    for first, last, shift in segments:
        low, high = bound_ref[first], bound_ref[last]
        full = (high - low) // BATCH

        def step(index, carry, low=low, shift=shift):
            move([low + index * BATCH + k for k in range(BATCH)], shift)
            return carry

        lax.fori_loop(0, full, step, 0)

        @pl.when(low + full * BATCH < high)
        def _(low=low, high=high, full=full, shift=shift):
            move([jnp.minimum(low + full * BATCH + k, high - 1) for k in range(BATCH)], shift)


def translate(start, picked, table_ref, tables_ref):
    at = pl.ds(start, CHUNK)
    per_row = table_ref.shape[1]
    coefs = tables_ref.shape[1]
    stride = 2 * per_row
    halves = [
        [
            picked[pl.ds(start * stride + 2 * k + h, CHUNK, stride=stride), :].astype(jnp.bfloat16)
            for h in range(2)
        ]
        for k in range(per_row)
    ]
    names = table_ref[at, :].astype(jnp.float32)
    named = [
        jnp.broadcast_to(names[:, k : k + 1], (CHUNK, LANES)).astype(jnp.bfloat16)
        for k in range(per_row)
    ]
    zero = jnp.zeros((CHUNK, LANES), jnp.bfloat16)
    total = jnp.zeros((CHUNK, coefs), jnp.float32)
    for t in range(tables_ref.shape[0]):
        chosen = [named[k] == jnp.bfloat16(t) for k in range(per_row)]
        mixed = []
        for h in range(2):
            value = jnp.where(chosen[0], halves[0][h], zero)
            for k in range(1, per_row):
                value = value + jnp.where(chosen[k], halves[k][h], zero)
            mixed.append(value)
        total = total + jnp.dot(
            jnp.concatenate(mixed, axis=1)[:, :coefs],
            tables_ref[t],
            preferred_element_type=jnp.float32,
        )
    return total


def row_chunks(rows, step, carry=0):
    return lax.fori_loop(
        0, rows // CHUNK, lambda i, c: step(pl.multiple_of(i * CHUNK, CHUNK), c), carry
    )


def terms_kernel(
    kind, segments, first, source_ref, target_ref, bound_ref, active_ref, table_ref, tables_ref, *rest
):
    *rest, source, picked = rest
    if kind == "near":
        incoming_ref, in_ref, angle_ref, *shards, out_ref = rest
    elif kind == "rest":
        part_ref, _, *shards, out_ref = rest
    elif kind in ("own", "some"):
        *shards, out_ref, done_ref = rest
        done_ref[...] = jnp.zeros_like(done_ref)
    else:
        *shards, out_ref = rest

    def part(index, carry):
        start = pl.multiple_of(index * CHUNK, CHUNK)
        at = pl.ds(start, CHUNK)
        total = translate(start, picked, table_ref, tables_ref)
        if kind == "near":
            total = total + spread_wave(at, incoming_ref, in_ref, angle_ref)
        if kind == "rest":
            total = total + part_ref[at, :]
        if out_ref.dtype == jnp.bfloat16:
            total = pad_lanes(total, out_ref.shape[1]).astype(jnp.bfloat16)
        out_ref[at, :] = total
        return carry

    @pl.when(active_ref[0] != 0)
    def _():
        load_rows(source, first, shards)
        pick_rows(source_ref, target_ref, bound_ref, segments, source, picked)
        lax.fori_loop(0, out_ref.shape[0] // CHUNK, part, 0)


def terms(kind, segments, first, requests, tables, shards, *extra, active=True):
    source, target, bounds, table_ids = requests
    rows, width = shards[0].shape
    coefs = tables.shape[1]
    if kind in ("near", "own"):
        outs = [jax.ShapeDtypeStruct((rows, coefs), jnp.float32)]
    else:
        outs = [jax.ShapeDtypeStruct((rows, width), jnp.bfloat16)]
    if kind in ("own", "some"):
        outs.append(jax.ShapeDtypeStruct((8, LANES), jnp.float32))
    return pl.pallas_call(
        functools.partial(terms_kernel, kind, segments, first),
        out_shape=tuple(outs),
        in_specs=[whole(pltpu.SMEM)] * 4 + [whole()] * (2 + len(extra) + len(shards)),
        out_specs=(whole(),) * len(outs),
        scratch_shapes=[
            pltpu.VMEM((2 * (first + len(shards)) * rows, LANES), jnp.float32),
            pltpu.VMEM((2 * source.shape[0], LANES), jnp.float32),
        ],
        compiler_params=params(),
        cost_estimate=COST,
        name="terms_" + kind,
    )(
        source,
        target,
        bounds,
        jnp.asarray(active).astype(jnp.int32).reshape(1),
        table_ids,
        tables,
        *extra,
        *shards,
    )


def join_kernel(second, count, base_ref, mie_ref, x_ref, *rest):
    served, rest = rest[:count], rest[count:]
    if second:
        vec_ref, sums_in_ref, *rest = rest
    else:
        vec_ref = x_ref
    image_ref, *rest, sums_ref = rest
    rows, coefs = base_ref.shape
    width = served[0].shape[1]

    def dot(a, b):
        return jnp.sum(a * b, axis=0, keepdims=True)

    def part(start, sums):
        at = pl.ds(start, CHUNK)
        far_rows = served[0][at, :].astype(jnp.float32)
        for other in served[1:]:
            far_rows = far_rows + other[at, :].astype(jnp.float32)
        image = pad_lanes(base_ref[at, :] + far_rows[:, :coefs], width).T[:coefs, :]
        image = mie_ref[:, at] * image
        image_ref[:, at] = image
        if not second:
            wide = jnp.concatenate([image, jnp.zeros((width - coefs, CHUNK), image.dtype)], axis=0)
            rest[0][at, :] = wide.T.astype(jnp.bfloat16)
        x, vec = x_ref[:, at], vec_ref[:, at]
        new = [dot(x, image), dot(vec, image) if second else dot(x, x), dot(image, image)]
        return tuple(a + b for a, b in zip(sums, new, strict=True))

    sums = row_chunks(rows, part, tuple(jnp.zeros((1, CHUNK), jnp.float32) for _ in range(3)))
    lane = lax.broadcasted_iota(jnp.int32, (1, LANES), 1)
    packed = sums_in_ref[...] if second else jnp.zeros((1, LANES), jnp.float32)
    for k, value in enumerate(sums):
        total = jnp.sum(value, axis=1, keepdims=True)
        packed = jnp.where(lane == k + (3 if second else 0), total, packed)
    sums_ref[...] = jnp.broadcast_to(packed, sums_ref.shape)


def join(base, mie_t, x_t, served, second=(), devices=1):
    rows, coefs = base.shape
    width = served[0].shape[1]
    outs = [jax.ShapeDtypeStruct((coefs, rows), jnp.float32)]
    if not second:
        outs.append(jax.ShapeDtypeStruct((rows, width), jnp.bfloat16))
    outs.append(jax.ShapeDtypeStruct((devices, LANES), jnp.float32))
    return pl.pallas_call(
        functools.partial(join_kernel, len(second) > 0, len(served)),
        out_shape=tuple(outs),
        in_specs=[whole()] * (3 + len(served) + len(second)),
        out_specs=(whole(),) * len(outs),
        compiler_params=params(),
        name="join_second" if second else "join_first",
    )(base, mie_t, x_t, *served, *second)


def finish_kernel(sums_ref, x_ref, b_ref, c_ref, solution_ref, residual_ref, hess_ref):
    sums = jnp.sum(sums_ref[...], axis=0, keepdims=True)
    xb, xx, bb, xc, bc, cc = [sums[:, k : k + 1] for k in range(6)]
    norm = jnp.sqrt(xx + epsilon)
    inverse = 1.0 / norm
    squared = inverse * inverse
    h11 = (xx - xb) * squared
    g = (xb + epsilon) * squared
    size1 = (g * g * xx - 2.0 * g * xb + bb) * squared
    h21 = jnp.sqrt(jnp.maximum(size1, 0.0) + epsilon)
    q = inverse / h21
    v11 = xx * squared
    v12 = q * inverse * (g * xx - xb)
    v22 = size1 / (h21 * h21)
    p1 = q * inverse * (g * xb - xc)
    p2 = q * q * (g * g * xb - g * xc - g * bb + bc)
    pp = q * q * (g * g * bb - 2.0 * g * bc + cc)
    h12 = v12 - p1
    h22 = v22 - p2
    rest = 1.0 - h22
    size2 = (
        rest * rest * v22
        + h12 * h12 * v11
        + pp
        - 2.0 * rest * h12 * v12
        - 2.0 * rest * p2
        + 2.0 * h12 * p1
    )
    h32 = jnp.sqrt(jnp.maximum(size2, 0.0) + epsilon)
    gram00 = h11 * h11 + h21 * h21
    gram01 = h11 * h12 + h21 * h22
    gram11 = h12 * h12 + h22 * h22 + h32 * h32
    rhs0, rhs1 = norm * h11, norm * h12
    det = gram00 * gram11 - gram01 * gram01
    a1 = (gram11 * rhs0 - gram01 * rhs1) / det * inverse
    a2 = (gram00 * rhs1 - gram01 * rhs0) / det * q
    x, b, c = x_ref[...], b_ref[...], c_ref[...]
    solution_ref[...] = (a1 + a2 * g) * x - a2 * b
    residual_ref[...] = (1.0 - a1 - a2 * g) * x + (a1 + a2 * (1.0 + g)) * b - a2 * c
    hess_ref[0:1, 0:1] = h11
    hess_ref[0:1, 1:2] = h21
    hess_ref[0:1, 2:3] = jnp.zeros_like(h11)
    hess_ref[1:2, 0:1] = h12
    hess_ref[1:2, 1:2] = h22
    hess_ref[1:2, 2:3] = h32


def finish(sums, x_t, b_t, c_t):
    field = jax.ShapeDtypeStruct(x_t.shape, jnp.float32)
    return pl.pallas_call(
        finish_kernel,
        out_shape=(field, field, jax.ShapeDtypeStruct((2, 3), jnp.float32)),
        in_specs=[whole()] * 4,
        out_specs=(whole(),) * 3,
        compiler_params=params(),
        name="finish",
    )(sums, x_t, b_t, c_t)


def flip(block, bits):
    return lax.ppermute(block, "grp", [(i, i ^ bits) for i in range(lax.axis_size("grp"))])


def along_chips(block, moves):
    return lax.ppermute(block, "grp", [(2 * a + c, 2 * b + c) for a, b in moves for c in range(2)])


def other_core(block, chips):
    return lax.ppermute(block, "grp", [(2 * z + c, 2 * z + 1 - c) for z in chips for c in range(2)])


def once(*values):
    return lax.optimization_barrier(values)


def wave_swaps(waves, count):
    blocks = lax.axis_size("blk")
    while waves.shape[0] < min(count, blocks):
        bits = waves.shape[0]
        moved = lax.ppermute(waves, "blk", [(i, i ^ bits) for i in range(blocks)])
        waves = jnp.concatenate([waves, moved], axis=0)
    return waves


def body(
    incident,
    mie_coef,
    owner_dev,
    near_row,
    table_id,
    tables,
    wave_out,
    wave_in,
    plane_angle,
    far_trans,
):
    x = incident[0]
    mie_t = mie_coef[0].T
    angle = plane_angle[0]
    rows, coefs = x.shape
    width = -(-coefs // LANES) * LANES
    group = lax.axis_size("grp")
    devices = group * lax.axis_size("blk")
    tables_count = tables.shape[0]
    wave_in_t = wave_in.T
    x_t = x.T

    apart = owner_dev[0, :, 0] ^ lax.axis_index("grp")
    count = apart.shape[0]
    bits = (count - 1).bit_length()
    number = jnp.arange(count, dtype=jnp.int32)
    listed = jnp.sort(((apart * rows + near_row[0]) << bits) | number)
    bounds = jnp.arange(group + 1, dtype=jnp.int32)
    bounds = jnp.sum((apart[None, :] < bounds[:, None]).astype(jnp.int32), axis=1)
    others = range(1, group // QUAD)

    def requests_of(message):
        word = message[:count]
        names = message[count : 2 * count].astype(jnp.bfloat16).reshape(rows, -1)
        source = 2 * ((word >> bits) % (QUAD * rows))
        return source, 2 * (word & ((1 << bits) - 1)), message[2 * count :], names

    message = jnp.concatenate([listed, table_id[0], bounds])
    asked = [flip(message, QUAD * j) for j in others]
    blocks = lax.axis_size("blk")
    turns = jnp.arange(blocks, dtype=jnp.int32)
    weights = far_trans[0, 0][turns ^ lax.axis_index("blk")]
    weights = jnp.where(turns[:, None] > 0, weights, 0.0)

    def incoming_of(waves):
        waves = wave_swaps(waves, blocks)
        return jnp.sum(weights * waves, axis=0, keepdims=True)

    coded = code(x_t, width)
    across, same = flip(coded, 2), flip(coded, 1)
    waves = gather_wave(coded, wave_out, angle)
    across, waves, *asked = once(across, waves, *asked)
    asked = [requests_of(words) for words in asked]
    local = requests_of(message)
    shards = [coded, same, across, flip(across, 1)]
    served = [
        flip(terms("all", ((QUAD * j, QUAD * j + QUAD, 0),), 0, words, tables, shards)[0], QUAD * j)
        for j, words in zip(others, asked, strict=True)
    ]
    base = terms("near", ((0, QUAD, 0),), 0, local, tables, shards, incoming_of(waves), wave_in_t, angle)[0]
    b_t, coded, sums = join(base, mie_t, x_t, served)

    def by_quads(coded):
        across, same = flip(coded, 2), flip(coded, 1)
        parts = [
            terms("own", ((QUAD * j, QUAD * j + 2, 0),), 0, words, tables, [coded, same])
            for j, words in zip(others, asked, strict=True)
        ]
        across, *done = once(across, *[done for _, done in parts])
        shards = [across, flip(across, 1)]
        served = [
            flip(
                terms("rest", ((QUAD * j + 2, QUAD * j + 4, 0),), 2, words, tables, shards, part, token)[0],
                QUAD * j,
            )
            for j, words, (part, _), token in zip(others, asked, parts, done, strict=True)
        ]
        incoming = incoming_of(gather_wave(coded, wave_out, angle))
        shards = [coded, same, *shards]
        return terms("near", ((0, QUAD, 0),), 0, local, tables, shards, incoming, wave_in_t, angle)[0], served

    def in_line(coded):
        chip = lax.axis_index("grp") // 2
        middle = (chip == 1) | (chip == 2)
        across = along_chips(coded, [(0, 1), (1, 0), (2, 3), (3, 2)])
        inner = along_chips(coded, [(1, 2), (2, 1)])
        same = flip(coded, 1)
        sums, done = terms(
            "some", ((QUAD, QUAD + 2, 0),), 0, asked[0], tables, [coded, same], active=~middle
        )
        early = along_chips(sums, [(0, 2), (3, 1)])
        waves = wave_swaps(gather_wave(coded, wave_out, angle), 2)
        across, inner, waves, done = once(across, inner, waves, done)
        shards = [coded, same, across, flip(across, 1)]
        active = middle & (done[0, 0] == 0.0)
        sums, done = terms(
            "some", ((QUAD, 2 * QUAD, 0),), 0, asked[0], tables, shards, active=active
        )
        late = along_chips(sums, [(1, 3), (2, 0)])
        inner, done = once(inner, done)
        incoming, early = once(incoming_of(waves), early)
        shards += [inner, other_core(inner, (1, 2))]
        source, target, bounds, names = local
        missing = (jnp.arange(group + 1) == 6) & ~middle
        requests = source, target, jnp.where(missing, bounds[8], bounds), names
        segments = ((0, QUAD, 0), (6, 8, 4 * rows))
        return terms("near", segments, 0, requests, tables, shards, incoming, wave_in_t, angle)[0], [early, late]

    base, served = by_quads(coded)
    c_t, sums = join(base, mie_t, x_t, served, (b_t, sums), devices)
    sums = lax.all_to_all(sums, ("blk", "grp"), 0, 0, tiled=True)
    solution_t, residual_t, hess_t = finish(sums, x_t, b_t, c_t)
    return solution_t.T[None], residual_t.T[None], hess_t.T


def solution(mesh):
    return jax.shard_map(
        body,
        mesh=mesh,
        in_specs=(
            P("blk", "grp", None),
            P("blk", "grp", None),
            P("blk", "grp", None),
            P("blk", "grp"),
            P("blk", "grp"),
            P(),
            P(),
            P(),
            P("blk", "grp", None),
            P("blk", "grp", None, None),
        ),
        out_specs=(P("blk", "grp", None), P("blk", "grp", None), P()),
        check_vma=False,
    )
```

```python
import functools

import jax
import jax.numpy as jnp
import numpy as np
from jax import lax
from jax.experimental import pallas as pl
from jax.experimental.pallas import tpu as pltpu
from jax.sharding import PartitionSpec as P

epsilon = 1e-06
LANES = 128
QUAD = 4
CHUNK = 512
BATCH = 32
VMEM_LIMIT = 16 * 2**20
COST = pl.CostEstimate(flops=1, bytes_accessed=1, transcendentals=0)


def cosine_coefficients():
    top = 3.1416**2
    nodes = (np.cos((np.arange(400) + 0.5) * np.pi / 400) + 1.0) * top / 2.0
    fit = np.polynomial.chebyshev.Chebyshev.fit(nodes, np.cos(np.sqrt(nodes)), 8, domain=[0.0, top])
    return [float(c) for c in fit.convert(kind=np.polynomial.Polynomial).coef]


COS = cosine_coefficients()


def cosine(angle):
    square = angle * angle
    value = jnp.full_like(square, COS[-1])
    for coef in COS[-2::-1]:
        value = value * square + coef
    return value


def whole(memory=pltpu.VMEM):
    return pl.BlockSpec(memory_space=memory)


def params():
    return pltpu.CompilerParams(vmem_limit_bytes=VMEM_LIMIT)


def pad_lanes(value, width):
    rows, cols = value.shape
    return jnp.concatenate([value, jnp.zeros((rows, width - cols), value.dtype)], axis=1)


def code_kernel(field_ref, *coded):
    coefs = field_ref.shape[0]
    start = 0
    for coded_ref in coded:
        rows, width = coded_ref.shape
        part = field_ref[:, pl.ds(start, rows)]
        part = jnp.concatenate([part, jnp.zeros((width - coefs, rows), part.dtype)], axis=0)
        coded_ref[...] = part.T.astype(jnp.bfloat16)
        start += rows


def code(field_t, width, cuts):
    return pl.pallas_call(
        code_kernel,
        out_shape=tuple(
            jax.ShapeDtypeStruct((stop - start, width), jnp.bfloat16) for start, stop in cuts
        ),
        in_specs=[whole()],
        out_specs=(whole(),) * len(cuts),
        compiler_params=params(),
        name="code_rows",
    )(field_t)


def wave_kernel(out_ref, angle_ref, *rest):
    *coded, sum_ref = rest
    coefs, samples = out_ref.shape
    total = jnp.zeros((1, samples), jnp.float32)
    start = 0
    for coded_ref in coded:
        rows = coded_ref.shape[0]
        outgoing = jnp.dot(
            coded_ref[...][:, :coefs], out_ref[...], preferred_element_type=jnp.float32
        )
        angle = angle_ref[pl.ds(start, rows), :].astype(jnp.float32)
        total = total + jnp.sum(cosine(angle) * outgoing, axis=0, keepdims=True)
        start += rows
    sum_ref[...] = total


def gather_wave(coded, wave_out, angle):
    samples = angle.shape[1]
    return pl.pallas_call(
        wave_kernel,
        out_shape=jax.ShapeDtypeStruct((1, samples), jnp.float32),
        in_specs=[whole()] * (2 + len(coded)),
        out_specs=whole(),
        compiler_params=params(),
        cost_estimate=COST,
        name="gather_wave",
    )(wave_out, angle, *coded)


def spread_wave(at, incoming_ref, in_ref, angle_ref):
    spread = cosine(angle_ref[at, :].astype(jnp.float32)) * incoming_ref[...]
    return lax.dot_general(
        spread.astype(jnp.bfloat16),
        in_ref[...],
        (((1,), (1,)), ((), ())),
        preferred_element_type=jnp.float32,
    )


def load_rows(source, stands, shards):
    for base, shard in zip(stands, shards, strict=True):
        value = shard[...].astype(jnp.float32)
        rows = value.shape[0]
        source[pl.ds(2 * base, rows, stride=2), :] = value[:, :LANES]
        source[pl.ds(2 * base + 1, rows, stride=2), :] = value[:, LANES:]


def pick_rows(source_ref, target_ref, bound_ref, segments, source, picked):
    def move(places):
        got = [source[pl.ds(pl.multiple_of(source_ref[n], 2), 2), :] for n in places]
        for n, row in zip(places, got, strict=True):
            picked[pl.ds(pl.multiple_of(target_ref[n], 2), 2), :] = row

    for first, last in segments:
        low, high = bound_ref[first], bound_ref[last]
        full = (high - low) // BATCH

        def step(index, carry, low=low):
            move([low + index * BATCH + k for k in range(BATCH)])
            return carry

        lax.fori_loop(0, full, step, 0)

        @pl.when(low + full * BATCH < high)
        def _(low=low, high=high, full=full):
            move([jnp.minimum(low + full * BATCH + k, high - 1) for k in range(BATCH)])


def translate(start, size, picked, table_ref, tables_ref):
    at = pl.ds(start, size)
    per_row = table_ref.shape[1]
    coefs = tables_ref.shape[1]
    stride = 2 * per_row
    halves = [
        [
            picked[pl.ds(start * stride + 2 * k + h, size, stride=stride), :].astype(jnp.bfloat16)
            for h in range(2)
        ]
        for k in range(per_row)
    ]
    names = table_ref[at, :].astype(jnp.float32)
    named = [
        jnp.broadcast_to(names[:, k : k + 1], (size, LANES)).astype(jnp.bfloat16)
        for k in range(per_row)
    ]
    zero = jnp.zeros((size, LANES), jnp.bfloat16)
    total = jnp.zeros((size, coefs), jnp.float32)
    for t in range(tables_ref.shape[0]):
        chosen = [named[k] == jnp.bfloat16(t) for k in range(per_row)]
        mixed = []
        for h in range(2):
            value = jnp.where(chosen[0], halves[0][h], zero)
            for k in range(1, per_row):
                value = value + jnp.where(chosen[k], halves[k][h], zero)
            mixed.append(value)
        total = total + jnp.dot(
            jnp.concatenate(mixed, axis=1)[:, :coefs],
            tables_ref[t],
            preferred_element_type=jnp.float32,
        )
    return total


def terms_kernel(
    kind, cut, segments, stands, source_ref, target_ref, bound_ref, table_ref, tables_ref, *rest
):
    *rest, source, picked = rest
    if kind == "own":
        *rest, done_ref = rest
        done_ref[...] = jnp.zeros_like(done_ref)
    *rest, out_ref = rest
    extra, shards = rest[: -len(stands)], rest[-len(stands) :]
    start, stop = cut
    load_rows(source, stands, shards)
    wide = 2 * table_ref.shape[1]
    cleared = pl.ds(start * wide, (stop - start) * wide)
    picked[cleared, :] = jnp.zeros(((stop - start) * wide, LANES), jnp.float32)
    pick_rows(source_ref, target_ref, bound_ref, segments, source, picked)
    size = min(CHUNK, stop - start)
    while (stop - start) % size:
        size += LANES
    for place in range(start, stop, size):
        at = pl.ds(place, size)
        total = translate(place, size, picked, table_ref, tables_ref)
        if kind == "near":
            total = total + spread_wave(at, *extra)
        if kind == "rest":
            total = total + extra[0][at, :]
        if kind in ("rest", "all"):
            total = pad_lanes(total, out_ref.shape[1]).astype(jnp.bfloat16)
        out_ref[pl.ds(place - start, size), :] = total


def terms(kind, cut, segments, blocks, requests, tables, *extra):
    source, target, bounds, table_ids = requests
    stands, shards = zip(*blocks, strict=True)
    rows, width = table_ids.shape[0], shards[0].shape[1]
    size = cut[1] - cut[0]
    if kind in ("near", "own"):
        outs = [jax.ShapeDtypeStruct((size, tables.shape[1]), jnp.float32)]
    else:
        outs = [jax.ShapeDtypeStruct((size, width), jnp.bfloat16)]
    if kind == "own":
        outs.append(jax.ShapeDtypeStruct((8, LANES), jnp.float32))
    return pl.pallas_call(
        functools.partial(terms_kernel, kind, cut, segments, stands),
        out_shape=tuple(outs),
        in_specs=[whole(pltpu.SMEM)] * 3 + [whole()] * (2 + len(extra) + len(shards)),
        out_specs=(whole(),) * len(outs),
        scratch_shapes=[
            pltpu.VMEM((2 * QUAD * rows, LANES), jnp.float32),
            pltpu.VMEM((2 * source.shape[0], LANES), jnp.float32),
        ],
        compiler_params=params(),
        cost_estimate=COST,
        name="terms_" + kind,
    )(source, target, bounds, table_ids, tables, *extra, *shards)


def join_kernel(cuts, count, base_ref, mie_ref, x_ref, sums_in_ref, *rest):
    served, rest = rest[: count * len(cuts)], rest[count * len(cuts) :]
    second = cuts[0][1] < cuts[-1][1]
    if second:
        old, rest = rest[: len(cuts)], rest[len(cuts) :]
    image_ref, *coded, sums_ref = rest
    coefs = base_ref.shape[1]
    width = served[0].shape[1]
    totals = [jnp.zeros((1, 1), jnp.float32)] * 3

    def dot(a, b):
        return jnp.sum(jnp.sum(a * b, axis=0, keepdims=True), axis=1, keepdims=True)

    for k, (start, stop) in enumerate(cuts):
        at = pl.ds(start, stop - start)
        here = served[k * count : (k + 1) * count]
        far_rows = here[0][...].astype(jnp.float32)
        for other in here[1:]:
            far_rows = far_rows + other[...].astype(jnp.float32)
        image = pad_lanes(base_ref[at, :] + far_rows[:, :coefs], width).T[:coefs, :]
        image = mie_ref[:, at] * image
        image_ref[:, pl.ds(start - cuts[0][0], stop - start)] = image
        x = x_ref[:, at]
        if second:
            new = [dot(x, image), dot(old[k][...], image), dot(image, image)]
        else:
            wide = jnp.concatenate([image, jnp.zeros((width - coefs, stop - start), image.dtype)], axis=0)
            coded[0][...] = wide.T.astype(jnp.bfloat16)
            new = [dot(x, image), dot(x, x), dot(image, image)]
        totals = [a + b for a, b in zip(totals, new, strict=True)]
    lane = lax.broadcasted_iota(jnp.int32, (1, LANES), 1)
    packed = sums_in_ref[...]
    for k, total in enumerate(totals):
        packed = packed + jnp.where(lane == k + (3 if second else 0), total, 0.0)
    sums_ref[...] = jnp.broadcast_to(packed, sums_ref.shape)


def join(cuts, base, mie_t, x_t, sums, served, old=(), devices=1):
    rows, coefs = base.shape
    size = cuts[-1][1] - cuts[0][0]
    outs = [jax.ShapeDtypeStruct((coefs, size), jnp.float32)]
    if not old:
        outs.append(jax.ShapeDtypeStruct((size, served[0].shape[1]), jnp.bfloat16))
    outs.append(jax.ShapeDtypeStruct((devices, LANES), jnp.float32))
    return pl.pallas_call(
        functools.partial(join_kernel, cuts, len(served) // len(cuts)),
        out_shape=tuple(outs),
        in_specs=[whole()] * (4 + len(served) + len(old)),
        out_specs=(whole(),) * len(outs),
        compiler_params=params(),
        name="join_second" if old else "join_first",
    )(base, mie_t, x_t, sums, *served, *old)


def finish_kernel(sums_ref, x_ref, c_ref, *rest):
    *parts, solution_ref, residual_ref, hess_ref = rest
    sums = jnp.sum(sums_ref[...], axis=0, keepdims=True)
    xb, xx, bb, xc, bc, cc = [sums[:, k : k + 1] for k in range(6)]
    norm = jnp.sqrt(xx + epsilon)
    inverse = 1.0 / norm
    squared = inverse * inverse
    h11 = (xx - xb) * squared
    g = (xb + epsilon) * squared
    size1 = (g * g * xx - 2.0 * g * xb + bb) * squared
    h21 = jnp.sqrt(jnp.maximum(size1, 0.0) + epsilon)
    q = inverse / h21
    v11 = xx * squared
    v12 = q * inverse * (g * xx - xb)
    v22 = size1 / (h21 * h21)
    p1 = q * inverse * (g * xb - xc)
    p2 = q * q * (g * g * xb - g * xc - g * bb + bc)
    pp = q * q * (g * g * bb - 2.0 * g * bc + cc)
    h12 = v12 - p1
    h22 = v22 - p2
    rest = 1.0 - h22
    size2 = (
        rest * rest * v22
        + h12 * h12 * v11
        + pp
        - 2.0 * rest * h12 * v12
        - 2.0 * rest * p2
        + 2.0 * h12 * p1
    )
    h32 = jnp.sqrt(jnp.maximum(size2, 0.0) + epsilon)
    gram00 = h11 * h11 + h21 * h21
    gram01 = h11 * h12 + h21 * h22
    gram11 = h12 * h12 + h22 * h22 + h32 * h32
    rhs0, rhs1 = norm * h11, norm * h12
    det = gram00 * gram11 - gram01 * gram01
    a1 = (gram11 * rhs0 - gram01 * rhs1) / det * inverse
    a2 = (gram00 * rhs1 - gram01 * rhs0) / det * q
    start = 0
    for b_ref in parts:
        at = pl.ds(start, b_ref.shape[1])
        x, b, c = x_ref[:, at], b_ref[...], c_ref[:, at]
        solution_ref[:, at] = (a1 + a2 * g) * x - a2 * b
        residual_ref[:, at] = (1.0 - a1 - a2 * g) * x + (a1 + a2 * (1.0 + g)) * b - a2 * c
        start += b_ref.shape[1]
    hess_ref[0:1, 0:1] = h11
    hess_ref[0:1, 1:2] = h21
    hess_ref[0:1, 2:3] = jnp.zeros_like(h11)
    hess_ref[1:2, 0:1] = h12
    hess_ref[1:2, 1:2] = h22
    hess_ref[1:2, 2:3] = h32


def finish(sums, x_t, c_t, parts):
    field = jax.ShapeDtypeStruct(x_t.shape, jnp.float32)
    return pl.pallas_call(
        finish_kernel,
        out_shape=(field, field, jax.ShapeDtypeStruct((2, 3), jnp.float32)),
        in_specs=[whole()] * (3 + len(parts)),
        out_specs=(whole(),) * 3,
        compiler_params=params(),
        name="finish",
    )(sums, x_t, c_t, *parts)


def flip(block, bits):
    return lax.ppermute(block, "grp", [(i, i ^ bits) for i in range(lax.axis_size("grp"))])


def once(*values):
    return lax.optimization_barrier(values)


def wave_swaps(waves, count):
    blocks = lax.axis_size("blk")
    while waves.shape[0] < min(count, blocks):
        bits = waves.shape[0]
        moved = lax.ppermute(waves, "blk", [(i, i ^ bits) for i in range(blocks)])
        waves = jnp.concatenate([waves, moved], axis=0)
    return waves


def body(
    incident,
    mie_coef,
    owner_dev,
    near_row,
    table_id,
    tables,
    wave_out,
    wave_in,
    plane_angle,
    far_trans,
):
    x = incident[0]
    mie_t = mie_coef[0].T
    angle = plane_angle[0]
    rows, coefs = x.shape
    width = -(-coefs // LANES) * LANES
    group = lax.axis_size("grp")
    devices = group * lax.axis_size("blk")
    tables_count = tables.shape[0]
    wave_in_t = wave_in.T
    x_t = x.T

    apart = owner_dev[0, :, 0] ^ lax.axis_index("grp")
    count = apart.shape[0]
    bits = (count - 1).bit_length()
    number = jnp.arange(count, dtype=jnp.int32)
    cuts = ((0, rows * 5 // 8), (rows * 5 // 8, rows))
    kind = jnp.where(number < cuts[0][1] * (count // rows), 0, group) + apart
    listed = jnp.sort(((kind * rows + near_row[0]) << bits) | number)
    bounds = jnp.arange(2 * group + 1, dtype=jnp.int32)
    bounds = jnp.sum((kind[None, :] < bounds[:, None]).astype(jnp.int32), axis=1)
    others = range(1, group // QUAD)

    def requests_of(message):
        word = message[:count]
        names = message[count : 2 * count].astype(jnp.bfloat16).reshape(rows, -1)
        source = 2 * ((word >> bits) % (QUAD * rows))
        return source, 2 * (word & ((1 << bits) - 1)), message[2 * count :], names

    message = jnp.concatenate([listed, table_id[0], bounds])
    asked = [flip(message, QUAD * j) for j in others]
    blocks = lax.axis_size("blk")
    turns = jnp.arange(blocks, dtype=jnp.int32)
    weights = far_trans[0, 0][turns ^ lax.axis_index("blk")]
    weights = jnp.where(turns[:, None] > 0, weights, 0.0)

    def incoming_of(waves):
        waves = wave_swaps(waves, blocks)
        return jnp.sum(weights * waves, axis=0, keepdims=True)

    def placed(first, *fields):
        return [
            ((first + place) * rows + start, block)
            for place, field in enumerate(fields)
            for (start, _), block in zip(cuts, field, strict=True)
        ]

    def near_of(shards, incoming):
        segments = ((0, QUAD), (group, group + QUAD))
        return terms("near", (0, rows), segments, shards, local, tables, incoming, wave_in_t, angle)[0]

    def swapped(blocks, bits):
        return [flip(block, bits) for block in blocks]

    coded = code(x_t, width, cuts)
    across, same = swapped(coded, 2), swapped(coded, 1)
    waves = gather_wave(coded, wave_out, angle)
    *across, waves, asked = once(*across, waves, asked)
    asked = [requests_of(words) for words in asked]
    local = requests_of(message)
    beyond = swapped(across, 1)
    shards = placed(0, coded, same, across, beyond)
    served = [
        [
            flip(
                terms(
                    "all",
                    cut,
                    ((part * group + QUAD * j, part * group + QUAD * j + QUAD),),
                    shards,
                    words,
                    tables,
                )[0],
                QUAD * j,
            )
            for j, words in zip(others, asked, strict=True)
        ]
        for part, cut in enumerate(cuts)
    ]
    base = near_of(shards, incoming_of(waves))
    b_t, coded, sums = [], [], jnp.zeros((1, LANES), jnp.float32)
    for cut, arrays in zip(cuts, served, strict=True):
        image, block, sums = join((cut,), base, mie_t, x_t, sums, arrays)
        b_t.append(image)
        coded.append(block)

    across, same = swapped(coded, 2), swapped(coded, 1)
    shards = placed(0, coded, same)
    own = [
        terms(
            "own",
            (0, rows),
            ((QUAD * j, QUAD * j + 2), (group + QUAD * j, group + QUAD * j + 2)),
            shards,
            words,
            tables,
        )
        for j, words in zip(others, asked, strict=True)
    ]
    *across, done = once(*across, [done for _, done in own])
    beyond = swapped(across, 1)
    shards = placed(2, across, beyond)
    served = [
        flip(
            terms(
                "rest",
                cut,
                ((part * group + QUAD * j + 2, part * group + QUAD * j + 4),),
                shards,
                words,
                tables,
                sums_here,
                token,
            )[0],
            QUAD * j,
        )
        for part, cut in enumerate(cuts)
        for j, words, (sums_here, _), token in zip(others, asked, own, done, strict=True)
    ]
    shards = placed(0, coded, same, across, beyond)
    base = near_of(shards, incoming_of(gather_wave(coded, wave_out, angle)))
    c_t, sums = join(cuts, base, mie_t, x_t, sums, served, b_t, devices)
    sums = lax.all_to_all(sums, ("blk", "grp"), 0, 0, tiled=True)
    solution_t, residual_t, hess_t = finish(sums, x_t, c_t, b_t)
    return solution_t.T[None], residual_t.T[None], hess_t.T


def solution(mesh):
    return jax.shard_map(
        body,
        mesh=mesh,
        in_specs=(
            P("blk", "grp", None),
            P("blk", "grp", None),
            P("blk", "grp", None),
            P("blk", "grp"),
            P("blk", "grp"),
            P(),
            P(),
            P(),
            P("blk", "grp", None),
            P("blk", "grp", None, None),
        ),
        out_specs=(P("blk", "grp", None), P("blk", "grp", None), P()),
        check_vma=False,
    )
```

```python
import functools

import jax
import jax.numpy as jnp
import numpy as np
from jax import lax
from jax.experimental import pallas as pl
from jax.experimental.pallas import tpu as pltpu
from jax.sharding import PartitionSpec as P

epsilon = 1e-06
LANES = 128
QUAD = 4
CHUNK = 512
BATCH = 32
VMEM_LIMIT = 16 * 2**20
COST = pl.CostEstimate(flops=1, bytes_accessed=1, transcendentals=0)


def cosine_coefficients():
    top = 3.1416**2
    nodes = (np.cos((np.arange(400) + 0.5) * np.pi / 400) + 1.0) * top / 2.0
    fit = np.polynomial.chebyshev.Chebyshev.fit(nodes, np.cos(np.sqrt(nodes)), 8, domain=[0.0, top])
    return [float(c) for c in fit.convert(kind=np.polynomial.Polynomial).coef]


COS = cosine_coefficients()


def cosine(angle):
    square = angle * angle
    value = jnp.full_like(square, COS[-1])
    for coef in COS[-2::-1]:
        value = value * square + coef
    return value


def whole(memory=pltpu.VMEM):
    return pl.BlockSpec(memory_space=memory)


def params():
    return pltpu.CompilerParams(vmem_limit_bytes=VMEM_LIMIT)


def pad_lanes(value, width):
    rows, cols = value.shape
    return jnp.concatenate([value, jnp.zeros((rows, width - cols), value.dtype)], axis=1)


def code_kernel(field_ref, *coded):
    coefs = field_ref.shape[0]
    start = 0
    for coded_ref in coded:
        rows, width = coded_ref.shape
        part = field_ref[:, pl.ds(start, rows)]
        part = jnp.concatenate([part, jnp.zeros((width - coefs, rows), part.dtype)], axis=0)
        coded_ref[...] = part.T.astype(jnp.bfloat16)
        start += rows


def code(field_t, width, cuts):
    return pl.pallas_call(
        code_kernel,
        out_shape=tuple(
            jax.ShapeDtypeStruct((stop - start, width), jnp.bfloat16) for start, stop in cuts
        ),
        in_specs=[whole()],
        out_specs=(whole(),) * len(cuts),
        compiler_params=params(),
        name="code_rows",
    )(field_t)


def wave_kernel(out_ref, angle_ref, *rest):
    *coded, sum_ref = rest
    coefs, samples = out_ref.shape
    total = jnp.zeros((1, samples), jnp.float32)
    start = 0
    for coded_ref in coded:
        rows = coded_ref.shape[0]
        outgoing = jnp.dot(
            coded_ref[...][:, :coefs], out_ref[...], preferred_element_type=jnp.float32
        )
        angle = angle_ref[pl.ds(start, rows), :].astype(jnp.float32)
        total = total + jnp.sum(cosine(angle) * outgoing, axis=0, keepdims=True)
        start += rows
    sum_ref[...] = total


def gather_wave(coded, wave_out, angle):
    samples = angle.shape[1]
    return pl.pallas_call(
        wave_kernel,
        out_shape=jax.ShapeDtypeStruct((1, samples), jnp.float32),
        in_specs=[whole()] * (2 + len(coded)),
        out_specs=whole(),
        compiler_params=params(),
        cost_estimate=COST,
        name="gather_wave",
    )(wave_out, angle, *coded)


def spread_wave(at, incoming_ref, in_ref, angle_ref):
    spread = cosine(angle_ref[at, :].astype(jnp.float32)) * incoming_ref[...]
    return lax.dot_general(
        spread.astype(jnp.bfloat16),
        in_ref[...],
        (((1,), (1,)), ((), ())),
        preferred_element_type=jnp.float32,
    )


def load_rows(source, stands, shards):
    for base, shard in zip(stands, shards, strict=True):
        value = shard[...].astype(jnp.float32)
        rows = value.shape[0]
        source[pl.ds(2 * base, rows, stride=2), :] = value[:, :LANES]
        source[pl.ds(2 * base + 1, rows, stride=2), :] = value[:, LANES:]


def pick_rows(source_ref, target_ref, bound_ref, segments, source, picked):
    def move(places):
        got = [source[pl.ds(pl.multiple_of(source_ref[n], 2), 2), :] for n in places]
        for n, row in zip(places, got, strict=True):
            picked[pl.ds(pl.multiple_of(target_ref[n], 2), 2), :] = row

    for first, last in segments:
        low, high = bound_ref[first], bound_ref[last]
        full = (high - low) // BATCH

        def step(index, carry, low=low):
            move([low + index * BATCH + k for k in range(BATCH)])
            return carry

        lax.fori_loop(0, full, step, 0)

        @pl.when(low + full * BATCH < high)
        def _(low=low, high=high, full=full):
            move([jnp.minimum(low + full * BATCH + k, high - 1) for k in range(BATCH)])


def translate(start, size, picked, table_ref, tables_ref):
    at = pl.ds(start, size)
    per_row = table_ref.shape[1]
    coefs = tables_ref.shape[1]
    stride = 2 * per_row
    halves = [
        [
            picked[pl.ds(start * stride + 2 * k + h, size, stride=stride), :].astype(jnp.bfloat16)
            for h in range(2)
        ]
        for k in range(per_row)
    ]
    names = table_ref[at, :].astype(jnp.float32)
    named = [
        jnp.broadcast_to(names[:, k : k + 1], (size, LANES)).astype(jnp.bfloat16)
        for k in range(per_row)
    ]
    zero = jnp.zeros((size, LANES), jnp.bfloat16)
    total = jnp.zeros((size, coefs), jnp.float32)
    for t in range(tables_ref.shape[0]):
        chosen = [named[k] == jnp.bfloat16(t) for k in range(per_row)]
        mixed = []
        for h in range(2):
            value = jnp.where(chosen[0], halves[0][h], zero)
            for k in range(1, per_row):
                value = value + jnp.where(chosen[k], halves[k][h], zero)
            mixed.append(value)
        total = total + jnp.dot(
            jnp.concatenate(mixed, axis=1)[:, :coefs],
            tables_ref[t],
            preferred_element_type=jnp.float32,
        )
    return total


def packed_rows(rows, coefs, width):
    kept = rows * coefs // width
    return kept, -(-kept // 16) * 16


def pack(value, width):
    rows, coefs = value.shape
    kept, stored = packed_rows(rows, coefs, width)
    gap = width - coefs
    wide = pad_lanes(value, width)
    last = wide[kept:]
    moved = []
    for lane in range(0, coefs, gap):
        half = last[:, lane // LANES * LANES :][:, :LANES]
        moved.append(pltpu.roll(half, (LANES - gap - lane) % LANES, 1))
    moved = jnp.concatenate(moved, axis=0)
    lanes = lax.broadcasted_iota(jnp.int32, moved.shape, 1)
    right = jnp.where(lanes < LANES - gap, wide[:kept, LANES:], moved)
    whole_rows = jnp.concatenate([wide[:kept, :LANES], right], axis=1)
    return jnp.concatenate([whole_rows, jnp.zeros((stored - kept, width), value.dtype)], axis=0)


def unpack(value, rows, coefs):
    width = value.shape[1]
    kept, _ = packed_rows(rows, coefs, width)
    gap, count = width - coefs, rows - kept
    halves = [jnp.zeros((count, LANES), value.dtype) for _ in range(width // LANES)]
    lanes = lax.broadcasted_iota(jnp.int32, (count, LANES), 1)
    for step, lane in enumerate(range(0, coefs, gap)):
        piece = value[step * count : (step + 1) * count, LANES:]
        low = lane % LANES
        piece = pltpu.roll(piece, (low - (LANES - gap)) % LANES, 1)
        here = (lanes >= low) & (lanes < low + gap)
        halves[lane // LANES] = jnp.where(here, piece, halves[lane // LANES])
    last = jnp.concatenate(halves, axis=1)
    return jnp.concatenate([value[:kept], last], axis=0)[:, :coefs]


def terms_kernel(
    kind, cut, segments, stands, source_ref, target_ref, bound_ref, table_ref, tables_ref, *rest
):
    *rest, source, picked = rest
    if kind == "own":
        *rest, done_ref = rest
        done_ref[...] = jnp.zeros_like(done_ref)
    *rest, out_ref = rest
    extra, shards = rest[: -len(stands)], rest[-len(stands) :]
    start, stop = cut
    load_rows(source, stands, shards)
    wide = 2 * table_ref.shape[1]
    cleared = pl.ds(start * wide, (stop - start) * wide)
    picked[cleared, :] = jnp.zeros(((stop - start) * wide, LANES), jnp.float32)
    pick_rows(source_ref, target_ref, bound_ref, segments, source, picked)
    size = CHUNK if kind in ("near", "own") else stop - start
    for place in range(start, stop, size):
        at = pl.ds(place, size)
        total = translate(place, size, picked, table_ref, tables_ref)
        if kind == "near":
            total = total + spread_wave(at, *extra)
        if kind == "rest":
            total = total + extra[0][at, :]
        if kind in ("rest", "all"):
            out_ref[...] = pack(total, out_ref.shape[1]).astype(jnp.bfloat16)
        else:
            out_ref[pl.ds(place - start, size), :] = total


def terms(kind, cut, segments, blocks, requests, tables, *extra):
    source, target, bounds, table_ids = requests
    stands, shards = zip(*blocks, strict=True)
    rows, width = table_ids.shape[0], shards[0].shape[1]
    size = cut[1] - cut[0]
    if kind in ("near", "own"):
        outs = [jax.ShapeDtypeStruct((size, tables.shape[1]), jnp.float32)]
    else:
        stored = packed_rows(size, tables.shape[1], width)[1]
        outs = [jax.ShapeDtypeStruct((stored, width), jnp.bfloat16)]
    if kind == "own":
        outs.append(jax.ShapeDtypeStruct((8, LANES), jnp.float32))
    return pl.pallas_call(
        functools.partial(terms_kernel, kind, cut, segments, stands),
        out_shape=tuple(outs),
        in_specs=[whole(pltpu.SMEM)] * 3 + [whole()] * (2 + len(extra) + len(shards)),
        out_specs=(whole(),) * len(outs),
        scratch_shapes=[
            pltpu.VMEM((2 * QUAD * rows, LANES), jnp.float32),
            pltpu.VMEM((2 * source.shape[0], LANES), jnp.float32),
        ],
        compiler_params=params(),
        cost_estimate=COST,
        name="terms_" + kind,
    )(source, target, bounds, table_ids, tables, *extra, *shards)


def join_kernel(cuts, count, base_ref, mie_ref, x_ref, sums_in_ref, *rest):
    served, rest = rest[: count * len(cuts)], rest[count * len(cuts) :]
    second = cuts[0][1] < cuts[-1][1]
    if second:
        old, rest = rest[: len(cuts)], rest[len(cuts) :]
    image_ref, *coded, sums_ref = rest
    coefs = base_ref.shape[1]
    width = served[0].shape[1]
    totals = [jnp.zeros((1, 1), jnp.float32)] * 3

    def dot(a, b):
        return jnp.sum(jnp.sum(a * b, axis=0, keepdims=True), axis=1, keepdims=True)

    for k, (start, stop) in enumerate(cuts):
        at = pl.ds(start, stop - start)
        here = served[k * count : (k + 1) * count]
        far_rows = here[0][...].astype(jnp.float32)
        for other in here[1:]:
            far_rows = far_rows + other[...].astype(jnp.float32)
        far_rows = unpack(far_rows, stop - start, coefs)
        image = pad_lanes(base_ref[at, :] + far_rows, width).T[:coefs, :]
        image = mie_ref[:, at] * image
        image_ref[:, pl.ds(start - cuts[0][0], stop - start)] = image
        x = x_ref[:, at]
        if second:
            new = [dot(x, image), dot(old[k][...], image), dot(image, image)]
        else:
            wide = jnp.concatenate([image, jnp.zeros((width - coefs, stop - start), image.dtype)], axis=0)
            coded[0][...] = wide.T.astype(jnp.bfloat16)
            new = [dot(x, image), dot(x, x), dot(image, image)]
        totals = [a + b for a, b in zip(totals, new, strict=True)]
    lane = lax.broadcasted_iota(jnp.int32, (1, LANES), 1)
    packed = sums_in_ref[...]
    for k, total in enumerate(totals):
        packed = packed + jnp.where(lane == k + (3 if second else 0), total, 0.0)
    sums_ref[...] = jnp.broadcast_to(packed, sums_ref.shape)


def join(cuts, base, mie_t, x_t, sums, served, old=(), devices=1):
    rows, coefs = base.shape
    size = cuts[-1][1] - cuts[0][0]
    outs = [jax.ShapeDtypeStruct((coefs, size), jnp.float32)]
    if not old:
        outs.append(jax.ShapeDtypeStruct((size, served[0].shape[1]), jnp.bfloat16))
    outs.append(jax.ShapeDtypeStruct((devices, LANES), jnp.float32))
    return pl.pallas_call(
        functools.partial(join_kernel, cuts, len(served) // len(cuts)),
        out_shape=tuple(outs),
        in_specs=[whole()] * (4 + len(served) + len(old)),
        out_specs=(whole(),) * len(outs),
        compiler_params=params(),
        name="join_second" if old else "join_first",
    )(base, mie_t, x_t, sums, *served, *old)


def finish_kernel(sums_ref, x_ref, c_ref, *rest):
    *parts, solution_ref, residual_ref, hess_ref = rest
    sums = jnp.sum(sums_ref[...], axis=0, keepdims=True)
    xb, xx, bb, xc, bc, cc = [sums[:, k : k + 1] for k in range(6)]
    norm = jnp.sqrt(xx + epsilon)
    inverse = 1.0 / norm
    squared = inverse * inverse
    h11 = (xx - xb) * squared
    g = (xb + epsilon) * squared
    size1 = (g * g * xx - 2.0 * g * xb + bb) * squared
    h21 = jnp.sqrt(jnp.maximum(size1, 0.0) + epsilon)
    q = inverse / h21
    v11 = xx * squared
    v12 = q * inverse * (g * xx - xb)
    v22 = size1 / (h21 * h21)
    p1 = q * inverse * (g * xb - xc)
    p2 = q * q * (g * g * xb - g * xc - g * bb + bc)
    pp = q * q * (g * g * bb - 2.0 * g * bc + cc)
    h12 = v12 - p1
    h22 = v22 - p2
    rest = 1.0 - h22
    size2 = (
        rest * rest * v22
        + h12 * h12 * v11
        + pp
        - 2.0 * rest * h12 * v12
        - 2.0 * rest * p2
        + 2.0 * h12 * p1
    )
    h32 = jnp.sqrt(jnp.maximum(size2, 0.0) + epsilon)
    gram00 = h11 * h11 + h21 * h21
    gram01 = h11 * h12 + h21 * h22
    gram11 = h12 * h12 + h22 * h22 + h32 * h32
    rhs0, rhs1 = norm * h11, norm * h12
    det = gram00 * gram11 - gram01 * gram01
    a1 = (gram11 * rhs0 - gram01 * rhs1) / det * inverse
    a2 = (gram00 * rhs1 - gram01 * rhs0) / det * q
    start = 0
    for b_ref in parts:
        at = pl.ds(start, b_ref.shape[1])
        x, b, c = x_ref[:, at], b_ref[...], c_ref[:, at]
        solution_ref[:, at] = (a1 + a2 * g) * x - a2 * b
        residual_ref[:, at] = (1.0 - a1 - a2 * g) * x + (a1 + a2 * (1.0 + g)) * b - a2 * c
        start += b_ref.shape[1]
    hess_ref[0:1, 0:1] = h11
    hess_ref[0:1, 1:2] = h21
    hess_ref[0:1, 2:3] = jnp.zeros_like(h11)
    hess_ref[1:2, 0:1] = h12
    hess_ref[1:2, 1:2] = h22
    hess_ref[1:2, 2:3] = h32


def finish(sums, x_t, c_t, parts):
    field = jax.ShapeDtypeStruct(x_t.shape, jnp.float32)
    return pl.pallas_call(
        finish_kernel,
        out_shape=(field, field, jax.ShapeDtypeStruct((2, 3), jnp.float32)),
        in_specs=[whole()] * (3 + len(parts)),
        out_specs=(whole(),) * 3,
        compiler_params=params(),
        name="finish",
    )(sums, x_t, c_t, *parts)


def flip(block, bits):
    return lax.ppermute(block, "grp", [(i, i ^ bits) for i in range(lax.axis_size("grp"))])


def once(*values):
    return lax.optimization_barrier(values)


def wave_swaps(waves, count):
    blocks = lax.axis_size("blk")
    while waves.shape[0] < min(count, blocks):
        bits = waves.shape[0]
        moved = lax.ppermute(waves, "blk", [(i, i ^ bits) for i in range(blocks)])
        waves = jnp.concatenate([waves, moved], axis=0)
    return waves


def body(
    incident,
    mie_coef,
    owner_dev,
    near_row,
    table_id,
    tables,
    wave_out,
    wave_in,
    plane_angle,
    far_trans,
):
    x = incident[0]
    mie_t = mie_coef[0].T
    angle = plane_angle[0]
    rows, coefs = x.shape
    width = -(-coefs // LANES) * LANES
    group = lax.axis_size("grp")
    devices = group * lax.axis_size("blk")
    tables_count = tables.shape[0]
    wave_in_t = wave_in.T
    x_t = x.T

    apart = owner_dev[0, :, 0] ^ lax.axis_index("grp")
    count = apart.shape[0]
    bits = (count - 1).bit_length()
    number = jnp.arange(count, dtype=jnp.int32)
    cuts = ((0, rows * 5 // 8), (rows * 5 // 8, rows))
    kind = jnp.where(number < cuts[0][1] * (count // rows), 0, group) + apart
    listed = jnp.sort(((kind * rows + near_row[0]) << bits) | number)
    bounds = jnp.arange(2 * group + 1, dtype=jnp.int32)
    bounds = jnp.sum((kind[None, :] < bounds[:, None]).astype(jnp.int32), axis=1)
    others = range(1, group // QUAD)

    def requests_of(message):
        word = message[:count]
        names = message[count : 2 * count].astype(jnp.bfloat16).reshape(rows, -1)
        source = 2 * ((word >> bits) % (QUAD * rows))
        return source, 2 * (word & ((1 << bits) - 1)), message[2 * count :], names

    message = jnp.concatenate([listed, table_id[0], bounds])
    asked = [flip(message, QUAD * j) for j in others]
    blocks = lax.axis_size("blk")
    turns = jnp.arange(blocks, dtype=jnp.int32)
    weights = far_trans[0, 0][turns ^ lax.axis_index("blk")]
    weights = jnp.where(turns[:, None] > 0, weights, 0.0)

    def incoming_of(waves):
        waves = wave_swaps(waves, blocks)
        return jnp.sum(weights * waves, axis=0, keepdims=True)

    def placed(first, *fields):
        return [
            ((first + place) * rows + start, block)
            for place, field in enumerate(fields)
            for (start, _), block in zip(cuts, field, strict=True)
        ]

    def near_of(shards, incoming):
        segments = ((0, QUAD), (group, group + QUAD))
        return terms("near", (0, rows), segments, shards, local, tables, incoming, wave_in_t, angle)[0]

    def swapped(blocks, bits):
        return [flip(block, bits) for block in blocks]

    coded = code(x_t, width, cuts)
    across, same = swapped(coded, 2), swapped(coded, 1)
    waves = gather_wave(coded, wave_out, angle)
    *across, waves, asked = once(*across, waves, asked)
    asked = [requests_of(words) for words in asked]
    local = requests_of(message)
    beyond = swapped(across, 1)
    shards = placed(0, coded, same, across, beyond)
    served = [
        [
            flip(
                terms(
                    "all",
                    cut,
                    ((part * group + QUAD * j, part * group + QUAD * j + QUAD),),
                    shards,
                    words,
                    tables,
                )[0],
                QUAD * j,
            )
            for j, words in zip(others, asked, strict=True)
        ]
        for part, cut in enumerate(cuts)
    ]
    base = near_of(shards, incoming_of(waves))
    b_t, coded, sums = [], [], jnp.zeros((1, LANES), jnp.float32)
    for cut, arrays in zip(cuts, served, strict=True):
        image, block, sums = join((cut,), base, mie_t, x_t, sums, arrays)
        b_t.append(image)
        coded.append(block)

    across, same = swapped(coded, 2), swapped(coded, 1)
    shards = placed(0, coded, same)
    own = [
        terms(
            "own",
            (0, rows),
            ((QUAD * j, QUAD * j + 2), (group + QUAD * j, group + QUAD * j + 2)),
            shards,
            words,
            tables,
        )
        for j, words in zip(others, asked, strict=True)
    ]
    *across, done = once(*across, [done for _, done in own])
    beyond = swapped(across, 1)
    shards = placed(2, across, beyond)
    served = [
        flip(
            terms(
                "rest",
                cut,
                ((part * group + QUAD * j + 2, part * group + QUAD * j + 4),),
                shards,
                words,
                tables,
                sums_here,
                token,
            )[0],
            QUAD * j,
        )
        for part, cut in enumerate(cuts)
        for j, words, (sums_here, _), token in zip(others, asked, own, done, strict=True)
    ]
    shards = placed(0, coded, same, across, beyond)
    base = near_of(shards, incoming_of(gather_wave(coded, wave_out, angle)))
    c_t, sums = join(cuts, base, mie_t, x_t, sums, served, b_t, devices)
    sums = lax.all_to_all(sums, ("blk", "grp"), 0, 0, tiled=True)
    solution_t, residual_t, hess_t = finish(sums, x_t, c_t, b_t)
    return solution_t.T[None], residual_t.T[None], hess_t.T


def solution(mesh):
    return jax.shard_map(
        body,
        mesh=mesh,
        in_specs=(
            P("blk", "grp", None),
            P("blk", "grp", None),
            P("blk", "grp", None),
            P("blk", "grp"),
            P("blk", "grp"),
            P(),
            P(),
            P(),
            P("blk", "grp", None),
            P("blk", "grp", None, None),
        ),
        out_specs=(P("blk", "grp", None), P("blk", "grp", None), P()),
        check_vma=False,
    )
```

```python
import functools

import jax
import jax.numpy as jnp
import numpy as np
from jax import lax
from jax.experimental import pallas as pl
from jax.experimental.pallas import tpu as pltpu
from jax.sharding import PartitionSpec as P

epsilon = 1e-06
LANES = 128
QUAD = 4
CHUNK = 512
BATCH = 32
VMEM_LIMIT = 16 * 2**20
COST = pl.CostEstimate(flops=1, bytes_accessed=1, transcendentals=0)


def cosine_coefficients():
    top = 3.1416**2
    nodes = (np.cos((np.arange(400) + 0.5) * np.pi / 400) + 1.0) * top / 2.0
    fit = np.polynomial.chebyshev.Chebyshev.fit(nodes, np.cos(np.sqrt(nodes)), 8, domain=[0.0, top])
    return [float(c) for c in fit.convert(kind=np.polynomial.Polynomial).coef]


COS = cosine_coefficients()


def cosine(angle):
    square = angle * angle
    value = jnp.full_like(square, COS[-1])
    for coef in COS[-2::-1]:
        value = value * square + coef
    return value


def whole(memory=pltpu.VMEM):
    return pl.BlockSpec(memory_space=memory)


def params():
    return pltpu.CompilerParams(vmem_limit_bytes=VMEM_LIMIT)


def pad_lanes(value, width):
    rows, cols = value.shape
    return jnp.concatenate([value, jnp.zeros((rows, width - cols), value.dtype)], axis=1)


def code_kernel(field_ref, *coded):
    coefs = field_ref.shape[0]
    start = 0
    for coded_ref in coded:
        rows, width = coded_ref.shape
        part = field_ref[:, pl.ds(start, rows)]
        part = jnp.concatenate([part, jnp.zeros((width - coefs, rows), part.dtype)], axis=0)
        coded_ref[...] = part.T.astype(jnp.bfloat16)
        start += rows


def code(field_t, width, cuts):
    return pl.pallas_call(
        code_kernel,
        out_shape=tuple(
            jax.ShapeDtypeStruct((stop - start, width), jnp.bfloat16) for start, stop in cuts
        ),
        in_specs=[whole()],
        out_specs=(whole(),) * len(cuts),
        compiler_params=params(),
        name="code_rows",
    )(field_t)


def wave_kernel(out_ref, angle_ref, *rest):
    *coded, sum_ref = rest
    coefs, samples = out_ref.shape
    total = jnp.zeros((1, samples), jnp.float32)
    start = 0
    for coded_ref in coded:
        rows = coded_ref.shape[0]
        outgoing = jnp.dot(
            coded_ref[...][:, :coefs], out_ref[...], preferred_element_type=jnp.float32
        )
        angle = angle_ref[pl.ds(start, rows), :].astype(jnp.float32)
        total = total + jnp.sum(cosine(angle) * outgoing, axis=0, keepdims=True)
        start += rows
    sum_ref[...] = total


def gather_wave(coded, wave_out, angle):
    samples = angle.shape[1]
    return pl.pallas_call(
        wave_kernel,
        out_shape=jax.ShapeDtypeStruct((1, samples), jnp.float32),
        in_specs=[whole()] * (2 + len(coded)),
        out_specs=whole(),
        compiler_params=params(),
        cost_estimate=COST,
        name="gather_wave",
    )(wave_out, angle, *coded)


def spread_wave(at, incoming_ref, in_ref, angle_ref):
    spread = cosine(angle_ref[at, :].astype(jnp.float32)) * incoming_ref[...]
    return lax.dot_general(
        spread.astype(jnp.bfloat16),
        in_ref[...],
        (((1,), (1,)), ((), ())),
        preferred_element_type=jnp.float32,
    )


def load_rows(source, stands, shards):
    for base, shard in zip(stands, shards, strict=True):
        value = shard[...].astype(jnp.float32)
        rows = value.shape[0]
        source[pl.ds(2 * base, rows, stride=2), :] = value[:, :LANES]
        source[pl.ds(2 * base + 1, rows, stride=2), :] = value[:, LANES:]


def pick_rows(source_ref, target_ref, bound_ref, segments, source, picked):
    def move(places):
        got = [source[pl.ds(pl.multiple_of(source_ref[n], 2), 2), :] for n in places]
        for n, row in zip(places, got, strict=True):
            picked[pl.ds(pl.multiple_of(target_ref[n], 2), 2), :] = row

    for first, last in segments:
        low, high = bound_ref[first], bound_ref[last]
        full = (high - low) // BATCH

        def step(index, carry, low=low):
            move([low + index * BATCH + k for k in range(BATCH)])
            return carry

        lax.fori_loop(0, full, step, 0)

        @pl.when(low + full * BATCH < high)
        def _(low=low, high=high, full=full):
            move([jnp.minimum(low + full * BATCH + k, high - 1) for k in range(BATCH)])


def translate(start, size, picked, table_ref, tables_ref):
    at = pl.ds(start, size)
    per_row = table_ref.shape[1]
    coefs = tables_ref.shape[1]
    stride = 2 * per_row
    halves = [
        [
            picked[pl.ds(start * stride + 2 * k + h, size, stride=stride), :].astype(jnp.bfloat16)
            for h in range(2)
        ]
        for k in range(per_row)
    ]
    names = table_ref[at, :].astype(jnp.float32)
    named = [
        jnp.broadcast_to(names[:, k : k + 1], (size, LANES)).astype(jnp.bfloat16)
        for k in range(per_row)
    ]
    zero = jnp.zeros((size, LANES), jnp.bfloat16)
    total = jnp.zeros((size, coefs), jnp.float32)
    for t in range(tables_ref.shape[0]):
        chosen = [named[k] == jnp.bfloat16(t) for k in range(per_row)]
        mixed = []
        for h in range(2):
            value = jnp.where(chosen[0], halves[0][h], zero)
            for k in range(1, per_row):
                value = value + jnp.where(chosen[k], halves[k][h], zero)
            mixed.append(value)
        total = total + jnp.dot(
            jnp.concatenate(mixed, axis=1)[:, :coefs],
            tables_ref[t],
            preferred_element_type=jnp.float32,
        )
    return total


def packed_rows(rows, coefs, width):
    kept = rows * coefs // width
    return kept, -(-kept // 16) * 16


def pack(value, width):
    rows, coefs = value.shape
    kept, stored = packed_rows(rows, coefs, width)
    gap = width - coefs
    wide = pad_lanes(value, width)
    last = wide[kept:]
    moved = []
    for lane in range(0, coefs, gap):
        half = last[:, lane // LANES * LANES :][:, :LANES]
        moved.append(pltpu.roll(half, (LANES - gap - lane) % LANES, 1))
    moved = jnp.concatenate(moved, axis=0)
    lanes = lax.broadcasted_iota(jnp.int32, moved.shape, 1)
    right = jnp.where(lanes < LANES - gap, wide[:kept, LANES:], moved)
    whole_rows = jnp.concatenate([wide[:kept, :LANES], right], axis=1)
    return jnp.concatenate([whole_rows, jnp.zeros((stored - kept, width), value.dtype)], axis=0)


def unpack(value, rows, coefs):
    width = value.shape[1]
    kept, _ = packed_rows(rows, coefs, width)
    gap, count = width - coefs, rows - kept
    halves = [jnp.zeros((count, LANES), value.dtype) for _ in range(width // LANES)]
    lanes = lax.broadcasted_iota(jnp.int32, (count, LANES), 1)
    for step, lane in enumerate(range(0, coefs, gap)):
        piece = value[step * count : (step + 1) * count, LANES:]
        low = lane % LANES
        piece = pltpu.roll(piece, (low - (LANES - gap)) % LANES, 1)
        here = (lanes >= low) & (lanes < low + gap)
        halves[lane // LANES] = jnp.where(here, piece, halves[lane // LANES])
    last = jnp.concatenate(halves, axis=1)
    return jnp.concatenate([value[:kept], last], axis=0)[:, :coefs]


def terms_kernel(
    kind, cut, segments, stands, source_ref, target_ref, bound_ref, table_ref, tables_ref, *rest
):
    *rest, source, picked = rest
    if kind == "own":
        *rest, done_ref = rest
        done_ref[...] = jnp.zeros_like(done_ref)
    *rest, out_ref = rest
    extra, shards = rest[: -len(stands)], rest[-len(stands) :]
    start, stop = cut
    load_rows(source, stands, shards)
    wide = 2 * table_ref.shape[1]
    cleared = pl.ds(start * wide, (stop - start) * wide)
    picked[cleared, :] = jnp.zeros(((stop - start) * wide, LANES), jnp.float32)
    pick_rows(source_ref, target_ref, bound_ref, segments, source, picked)
    size = CHUNK if kind in ("near", "own") else stop - start
    for place in range(start, stop, size):
        at = pl.ds(place, size)
        total = translate(place, size, picked, table_ref, tables_ref)
        if kind == "near":
            total = total + spread_wave(at, *extra)
        if kind == "rest":
            total = total + extra[0][at, :]
        if kind in ("rest", "all"):
            out_ref[...] = pack(total, out_ref.shape[1]).astype(jnp.bfloat16)
        else:
            out_ref[pl.ds(place - start, size), :] = total


def terms(kind, cut, segments, blocks, requests, tables, *extra):
    source, target, bounds, table_ids = requests
    stands, shards = zip(*blocks, strict=True)
    rows, width = table_ids.shape[0], shards[0].shape[1]
    size = cut[1] - cut[0]
    if kind in ("near", "own"):
        outs = [jax.ShapeDtypeStruct((size, tables.shape[1]), jnp.float32)]
    else:
        stored = packed_rows(size, tables.shape[1], width)[1]
        outs = [jax.ShapeDtypeStruct((stored, width), jnp.bfloat16)]
    if kind == "own":
        outs.append(jax.ShapeDtypeStruct((8, LANES), jnp.float32))
    return pl.pallas_call(
        functools.partial(terms_kernel, kind, cut, segments, stands),
        out_shape=tuple(outs),
        in_specs=[whole(pltpu.SMEM)] * 3 + [whole()] * (2 + len(extra) + len(shards)),
        out_specs=(whole(),) * len(outs),
        scratch_shapes=[
            pltpu.VMEM((2 * QUAD * rows + 8, LANES), jnp.float32),
            pltpu.VMEM((2 * source.shape[0] + 8, LANES), jnp.float32),
        ],
        compiler_params=params(),
        cost_estimate=COST,
        name="terms_" + kind,
    )(source, target, bounds, table_ids, tables, *extra, *shards)


def join_kernel(cuts, count, base_ref, mie_ref, x_ref, sums_in_ref, *rest):
    served, rest = rest[: count * len(cuts)], rest[count * len(cuts) :]
    second = cuts[0][1] < cuts[-1][1]
    if second:
        old, rest = rest[: len(cuts)], rest[len(cuts) :]
    image_ref, *coded, sums_ref = rest
    coefs = base_ref.shape[1]
    width = served[0].shape[1]
    totals = [jnp.zeros((1, 1), jnp.float32)] * 3

    def dot(a, b):
        return jnp.sum(jnp.sum(a * b, axis=0, keepdims=True), axis=1, keepdims=True)

    for k, (start, stop) in enumerate(cuts):
        at = pl.ds(start, stop - start)
        here = served[k * count : (k + 1) * count]
        far_rows = here[0][...].astype(jnp.float32)
        for other in here[1:]:
            far_rows = far_rows + other[...].astype(jnp.float32)
        far_rows = unpack(far_rows, stop - start, coefs)
        image = pad_lanes(base_ref[at, :] + far_rows, width).T[:coefs, :]
        image = mie_ref[:, at] * image
        image_ref[:, pl.ds(start - cuts[0][0], stop - start)] = image
        x = x_ref[:, at]
        if second:
            new = [dot(x, image), dot(old[k][...], image), dot(image, image)]
        else:
            wide = jnp.concatenate([image, jnp.zeros((width - coefs, stop - start), image.dtype)], axis=0)
            coded[0][...] = wide.T.astype(jnp.bfloat16)
            new = [dot(x, image), dot(x, x), dot(image, image)]
        totals = [a + b for a, b in zip(totals, new, strict=True)]
    lane = lax.broadcasted_iota(jnp.int32, (1, LANES), 1)
    packed = sums_in_ref[...]
    for k, total in enumerate(totals):
        packed = packed + jnp.where(lane == k + (3 if second else 0), total, 0.0)
    sums_ref[...] = jnp.broadcast_to(packed, sums_ref.shape)


def join(cuts, base, mie_t, x_t, sums, served, old=(), devices=1):
    rows, coefs = base.shape
    size = cuts[-1][1] - cuts[0][0]
    outs = [jax.ShapeDtypeStruct((coefs, size), jnp.float32)]
    if not old:
        outs.append(jax.ShapeDtypeStruct((size, served[0].shape[1]), jnp.bfloat16))
    outs.append(jax.ShapeDtypeStruct((devices, LANES), jnp.float32))
    return pl.pallas_call(
        functools.partial(join_kernel, cuts, len(served) // len(cuts)),
        out_shape=tuple(outs),
        in_specs=[whole()] * (4 + len(served) + len(old)),
        out_specs=(whole(),) * len(outs),
        compiler_params=params(),
        name="join_second" if old else "join_first",
    )(base, mie_t, x_t, sums, *served, *old)


def finish_kernel(sums_ref, x_ref, c_ref, *rest):
    *parts, solution_ref, residual_ref, hess_ref = rest
    sums = jnp.sum(sums_ref[...], axis=0, keepdims=True)
    xb, xx, bb, xc, bc, cc = [sums[:, k : k + 1] for k in range(6)]
    norm = jnp.sqrt(xx + epsilon)
    inverse = 1.0 / norm
    squared = inverse * inverse
    h11 = (xx - xb) * squared
    g = (xb + epsilon) * squared
    size1 = (g * g * xx - 2.0 * g * xb + bb) * squared
    h21 = jnp.sqrt(jnp.maximum(size1, 0.0) + epsilon)
    q = inverse / h21
    v11 = xx * squared
    v12 = q * inverse * (g * xx - xb)
    v22 = size1 / (h21 * h21)
    p1 = q * inverse * (g * xb - xc)
    p2 = q * q * (g * g * xb - g * xc - g * bb + bc)
    pp = q * q * (g * g * bb - 2.0 * g * bc + cc)
    h12 = v12 - p1
    h22 = v22 - p2
    rest = 1.0 - h22
    size2 = (
        rest * rest * v22
        + h12 * h12 * v11
        + pp
        - 2.0 * rest * h12 * v12
        - 2.0 * rest * p2
        + 2.0 * h12 * p1
    )
    h32 = jnp.sqrt(jnp.maximum(size2, 0.0) + epsilon)
    gram00 = h11 * h11 + h21 * h21
    gram01 = h11 * h12 + h21 * h22
    gram11 = h12 * h12 + h22 * h22 + h32 * h32
    rhs0, rhs1 = norm * h11, norm * h12
    det = gram00 * gram11 - gram01 * gram01
    a1 = (gram11 * rhs0 - gram01 * rhs1) / det * inverse
    a2 = (gram00 * rhs1 - gram01 * rhs0) / det * q
    start = 0
    for b_ref in parts:
        at = pl.ds(start, b_ref.shape[1])
        x, b, c = x_ref[:, at], b_ref[...], c_ref[:, at]
        solution_ref[:, at] = (a1 + a2 * g) * x - a2 * b
        residual_ref[:, at] = (1.0 - a1 - a2 * g) * x + (a1 + a2 * (1.0 + g)) * b - a2 * c
        start += b_ref.shape[1]
    hess_ref[0:1, 0:1] = h11
    hess_ref[0:1, 1:2] = h21
    hess_ref[0:1, 2:3] = jnp.zeros_like(h11)
    hess_ref[1:2, 0:1] = h12
    hess_ref[1:2, 1:2] = h22
    hess_ref[1:2, 2:3] = h32


def finish(sums, x_t, c_t, parts):
    field = jax.ShapeDtypeStruct(x_t.shape, jnp.float32)
    return pl.pallas_call(
        finish_kernel,
        out_shape=(field, field, jax.ShapeDtypeStruct((2, 3), jnp.float32)),
        in_specs=[whole()] * (3 + len(parts)),
        out_specs=(whole(),) * 3,
        compiler_params=params(),
        name="finish",
    )(sums, x_t, c_t, *parts)


def flip(block, bits):
    return lax.ppermute(block, "grp", [(i, i ^ bits) for i in range(lax.axis_size("grp"))])


def once(*values):
    return lax.optimization_barrier(values)


def wave_swaps(waves, count):
    blocks = lax.axis_size("blk")
    while waves.shape[0] < min(count, blocks):
        bits = waves.shape[0]
        moved = lax.ppermute(waves, "blk", [(i, i ^ bits) for i in range(blocks)])
        waves = jnp.concatenate([waves, moved], axis=0)
    return waves


def body(
    incident,
    mie_coef,
    owner_dev,
    near_row,
    table_id,
    tables,
    wave_out,
    wave_in,
    plane_angle,
    far_trans,
):
    x = incident[0]
    mie_t = mie_coef[0].T
    angle = plane_angle[0]
    rows, coefs = x.shape
    width = -(-coefs // LANES) * LANES
    group = lax.axis_size("grp")
    devices = group * lax.axis_size("blk")
    tables_count = tables.shape[0]
    wave_in_t = wave_in.T
    x_t = x.T

    apart = owner_dev[0, :, 0] ^ lax.axis_index("grp")
    count = apart.shape[0]
    bits = (count - 1).bit_length()
    number = jnp.arange(count, dtype=jnp.int32)
    cuts = ((0, rows * 5 // 8), (rows * 5 // 8, rows))
    kind = jnp.where(number < cuts[0][1] * (count // rows), 0, group) + apart
    listed = jnp.sort(((kind * rows + near_row[0]) << bits) | number)
    bounds = jnp.arange(2 * group + 1, dtype=jnp.int32)
    bounds = jnp.sum((kind[None, :] < bounds[:, None]).astype(jnp.int32), axis=1)
    others = range(1, group // QUAD)

    def requests_of(message):
        word = message[:count]
        names = message[count : 2 * count].astype(jnp.bfloat16).reshape(rows, -1)
        source = 2 * ((word >> bits) % (QUAD * rows))
        return source, 2 * (word & ((1 << bits) - 1)), message[2 * count :], names

    message = jnp.concatenate([listed, table_id[0], bounds])
    asked = [flip(message, QUAD * j) for j in others]
    blocks = lax.axis_size("blk")
    turns = jnp.arange(blocks, dtype=jnp.int32)
    weights = far_trans[0, 0][turns ^ lax.axis_index("blk")]
    weights = jnp.where(turns[:, None] > 0, weights, 0.0)

    def incoming_of(waves):
        waves = wave_swaps(waves, blocks)
        return jnp.sum(weights * waves, axis=0, keepdims=True)

    def placed(first, *fields):
        return [
            ((first + place) * rows + start, block)
            for place, field in enumerate(fields)
            for (start, _), block in zip(cuts, field, strict=True)
        ]

    def near_of(shards, incoming):
        segments = ((0, QUAD), (group, group + QUAD))
        return terms("near", (0, rows), segments, shards, local, tables, incoming, wave_in_t, angle)[0]

    def swapped(blocks, bits):
        return [flip(block, bits) for block in blocks]

    coded = code(x_t, width, cuts)
    across, same = swapped(coded, 2), swapped(coded, 1)
    waves = gather_wave(coded, wave_out, angle)
    *across, waves, asked = once(*across, waves, asked)
    asked = [requests_of(words) for words in asked]
    local = requests_of(message)
    beyond = swapped(across, 1)
    shards = placed(0, coded, same, across, beyond)
    served = [
        [
            flip(
                terms(
                    "all",
                    cut,
                    ((part * group + QUAD * j, part * group + QUAD * j + QUAD),),
                    shards,
                    words,
                    tables,
                )[0],
                QUAD * j,
            )
            for j, words in zip(others, asked, strict=True)
        ]
        for part, cut in enumerate(cuts)
    ]
    base = near_of(shards, incoming_of(waves))
    b_t, coded, sums = [], [], jnp.zeros((1, LANES), jnp.float32)
    for cut, arrays in zip(cuts, served, strict=True):
        image, block, sums = join((cut,), base, mie_t, x_t, sums, arrays)
        b_t.append(image)
        coded.append(block)

    across, same = swapped(coded, 2), swapped(coded, 1)
    shards = placed(0, coded, same)
    own = [
        terms(
            "own",
            (0, rows),
            ((QUAD * j, QUAD * j + 2), (group + QUAD * j, group + QUAD * j + 2)),
            shards,
            words,
            tables,
        )
        for j, words in zip(others, asked, strict=True)
    ]
    *across, done = once(*across, [done for _, done in own])
    beyond = swapped(across, 1)
    shards = placed(2, across, beyond)
    served = [
        flip(
            terms(
                "rest",
                cut,
                ((part * group + QUAD * j + 2, part * group + QUAD * j + 4),),
                shards,
                words,
                tables,
                sums_here,
                token,
            )[0],
            QUAD * j,
        )
        for part, cut in enumerate(cuts)
        for j, words, (sums_here, _), token in zip(others, asked, own, done, strict=True)
    ]
    shards = placed(0, coded, same, across, beyond)
    base = near_of(shards, incoming_of(gather_wave(coded, wave_out, angle)))
    c_t, sums = join(cuts, base, mie_t, x_t, sums, served, b_t, devices)
    sums = lax.all_to_all(sums, ("blk", "grp"), 0, 0, tiled=True)
    solution_t, residual_t, hess_t = finish(sums, x_t, c_t, b_t)
    return solution_t.T[None], residual_t.T[None], hess_t.T


def solution(mesh):
    return jax.shard_map(
        body,
        mesh=mesh,
        in_specs=(
            P("blk", "grp", None),
            P("blk", "grp", None),
            P("blk", "grp", None),
            P("blk", "grp"),
            P("blk", "grp"),
            P(),
            P(),
            P(),
            P("blk", "grp", None),
            P("blk", "grp", None, None),
        ),
        out_specs=(P("blk", "grp", None), P("blk", "grp", None), P()),
        check_vma=False,
    )
```

```python
import functools

import jax
import jax.numpy as jnp
import numpy as np
from jax import lax
from jax.experimental import pallas as pl
from jax.experimental.pallas import tpu as pltpu
from jax.sharding import PartitionSpec as P

epsilon = 1e-06
LANES = 128
QUAD = 4
CHUNK = 512
BATCH = 32
VMEM_LIMIT = 16 * 2**20
COST = pl.CostEstimate(flops=1, bytes_accessed=1, transcendentals=0)


def cosine_coefficients():
    top = 3.1416**2
    nodes = (np.cos((np.arange(400) + 0.5) * np.pi / 400) + 1.0) * top / 2.0
    fit = np.polynomial.chebyshev.Chebyshev.fit(nodes, np.cos(np.sqrt(nodes)), 8, domain=[0.0, top])
    return [float(c) for c in fit.convert(kind=np.polynomial.Polynomial).coef]


COS = cosine_coefficients()


def cosine(angle):
    square = angle * angle
    value = jnp.full_like(square, COS[-1])
    for coef in COS[-2::-1]:
        value = value * square + coef
    return value


def whole(memory=pltpu.VMEM):
    return pl.BlockSpec(memory_space=memory)


def params():
    return pltpu.CompilerParams(vmem_limit_bytes=VMEM_LIMIT)


def pad_lanes(value, width):
    rows, cols = value.shape
    return jnp.concatenate([value, jnp.zeros((rows, width - cols), value.dtype)], axis=1)


def code_kernel(field_ref, *coded):
    coefs = field_ref.shape[0]
    start = 0
    for coded_ref in coded:
        rows, width = coded_ref.shape
        part = field_ref[:, pl.ds(start, rows)]
        part = jnp.concatenate([part, jnp.zeros((width - coefs, rows), part.dtype)], axis=0)
        coded_ref[...] = part.T.astype(jnp.bfloat16)
        start += rows


def code(field_t, width, cuts):
    return pl.pallas_call(
        code_kernel,
        out_shape=tuple(
            jax.ShapeDtypeStruct((stop - start, width), jnp.bfloat16) for start, stop in cuts
        ),
        in_specs=[whole()],
        out_specs=(whole(),) * len(cuts),
        compiler_params=params(),
        name="code_rows",
    )(field_t)


def wave_kernel(out_ref, angle_ref, *rest):
    *coded, sum_ref = rest
    coefs, samples = out_ref.shape
    total = jnp.zeros((1, samples), jnp.float32)
    start = 0
    for coded_ref in coded:
        rows = coded_ref.shape[0]
        outgoing = jnp.dot(
            coded_ref[...][:, :coefs], out_ref[...], preferred_element_type=jnp.float32
        )
        angle = angle_ref[pl.ds(start, rows), :].astype(jnp.float32)
        total = total + jnp.sum(cosine(angle) * outgoing, axis=0, keepdims=True)
        start += rows
    sum_ref[...] = total


def gather_wave(coded, wave_out, angle):
    samples = angle.shape[1]
    return pl.pallas_call(
        wave_kernel,
        out_shape=jax.ShapeDtypeStruct((1, samples), jnp.float32),
        in_specs=[whole()] * (2 + len(coded)),
        out_specs=whole(),
        compiler_params=params(),
        cost_estimate=COST,
        name="gather_wave",
    )(wave_out, angle, *coded)


def spread_wave(at, incoming_ref, in_ref, angle_ref):
    spread = cosine(angle_ref[at, :].astype(jnp.float32)) * incoming_ref[...]
    return lax.dot_general(
        spread.astype(jnp.bfloat16),
        in_ref[...],
        (((1,), (1,)), ((), ())),
        preferred_element_type=jnp.float32,
    )


def load_rows(source, stands, shards):
    for base, shard in zip(stands, shards, strict=True):
        value = shard[...].astype(jnp.float32)
        rows = value.shape[0]
        source[pl.ds(2 * base, rows, stride=2), :] = value[:, :LANES]
        source[pl.ds(2 * base + 1, rows, stride=2), :] = value[:, LANES:]


def pick_rows(source_ref, target_ref, bound_ref, segments, source, picked):
    def move(places):
        got = [source[pl.ds(pl.multiple_of(source_ref[n], 2), 2), :] for n in places]
        for n, row in zip(places, got, strict=True):
            picked[pl.ds(pl.multiple_of(target_ref[n], 2), 2), :] = row

    for first, last in segments:
        low, high = bound_ref[first], bound_ref[last]
        full = (high - low) // BATCH

        def step(index, carry, low=low):
            move([low + index * BATCH + k for k in range(BATCH)])
            return carry

        lax.fori_loop(0, full, step, 0)

        @pl.when(low + full * BATCH < high)
        def _(low=low, high=high, full=full):
            move([jnp.minimum(low + full * BATCH + k, high - 1) for k in range(BATCH)])


def translate(start, size, picked, table_ref, tables_ref):
    at = pl.ds(start, size)
    per_row = table_ref.shape[1]
    coefs = tables_ref.shape[1]
    stride = 2 * per_row
    halves = [
        [
            picked[pl.ds(start * stride + 2 * k + h, size, stride=stride), :].astype(jnp.bfloat16)
            for h in range(2)
        ]
        for k in range(per_row)
    ]
    names = table_ref[at, :].astype(jnp.float32)
    named = [
        jnp.broadcast_to(names[:, k : k + 1], (size, LANES)).astype(jnp.bfloat16)
        for k in range(per_row)
    ]
    zero = jnp.zeros((size, LANES), jnp.bfloat16)
    total = jnp.zeros((size, coefs), jnp.float32)
    for t in range(tables_ref.shape[0]):
        chosen = [named[k] == jnp.bfloat16(t) for k in range(per_row)]
        mixed = []
        for h in range(2):
            value = jnp.where(chosen[0], halves[0][h], zero)
            for k in range(1, per_row):
                value = value + jnp.where(chosen[k], halves[k][h], zero)
            mixed.append(value)
        total = total + jnp.dot(
            jnp.concatenate(mixed, axis=1)[:, :coefs],
            tables_ref[t],
            preferred_element_type=jnp.float32,
        )
    return total


def packed_rows(rows, coefs, width):
    kept = rows * coefs // width
    return kept, -(-kept // 16) * 16


def pack(value, width):
    rows, coefs = value.shape
    kept, stored = packed_rows(rows, coefs, width)
    gap = width - coefs
    wide = pad_lanes(value, width)
    last = wide[kept:]
    moved = []
    for lane in range(0, coefs, gap):
        half = last[:, lane // LANES * LANES :][:, :LANES]
        moved.append(pltpu.roll(half, (LANES - gap - lane) % LANES, 1))
    moved = jnp.concatenate(moved, axis=0)
    lanes = lax.broadcasted_iota(jnp.int32, moved.shape, 1)
    right = jnp.where(lanes < LANES - gap, wide[:kept, LANES:], moved)
    whole_rows = jnp.concatenate([wide[:kept, :LANES], right], axis=1)
    return jnp.concatenate([whole_rows, jnp.zeros((stored - kept, width), value.dtype)], axis=0)


def unpack(value, rows, coefs):
    width = value.shape[1]
    kept, _ = packed_rows(rows, coefs, width)
    gap, count = width - coefs, rows - kept
    halves = [jnp.zeros((count, LANES), value.dtype) for _ in range(width // LANES)]
    lanes = lax.broadcasted_iota(jnp.int32, (count, LANES), 1)
    for step, lane in enumerate(range(0, coefs, gap)):
        piece = value[step * count : (step + 1) * count, LANES:]
        low = lane % LANES
        piece = pltpu.roll(piece, (low - (LANES - gap)) % LANES, 1)
        here = (lanes >= low) & (lanes < low + gap)
        halves[lane // LANES] = jnp.where(here, piece, halves[lane // LANES])
    last = jnp.concatenate(halves, axis=1)
    return jnp.concatenate([value[:kept], last], axis=0)[:, :coefs]


def terms_kernel(
    kind, cut, segments, stands, source_ref, target_ref, bound_ref, table_ref, tables_ref, *rest
):
    *rest, source, picked = rest
    if kind == "own":
        *rest, done_ref = rest
        done_ref[...] = jnp.zeros_like(done_ref)
    *rest, out_ref = rest
    extra, shards = rest[: -len(stands)], rest[-len(stands) :]
    start, stop = cut
    load_rows(source, stands, shards)
    wide = 2 * table_ref.shape[1]
    cleared = pl.ds(start * wide, (stop - start) * wide)
    picked[cleared, :] = jnp.zeros(((stop - start) * wide, LANES), jnp.float32)
    pick_rows(source_ref, target_ref, bound_ref, segments, source, picked)
    size = CHUNK if kind in ("near", "own") else stop - start
    for place in range(start, stop, size):
        at = pl.ds(place, size)
        total = translate(place, size, picked, table_ref, tables_ref)
        if kind == "near":
            total = total + spread_wave(at, *extra)
        if kind == "rest":
            total = total + extra[0][at, :]
        if kind in ("rest", "all"):
            out_ref[...] = pack(total, out_ref.shape[1]).astype(jnp.bfloat16)
        else:
            out_ref[pl.ds(place - start, size), :] = total


def terms(kind, cut, segments, blocks, requests, tables, *extra):
    source, target, bounds, table_ids = requests
    stands, shards = zip(*blocks, strict=True)
    rows, width = table_ids.shape[0], shards[0].shape[1]
    size = cut[1] - cut[0]
    if kind in ("near", "own"):
        outs = [jax.ShapeDtypeStruct((size, tables.shape[1]), jnp.float32)]
    else:
        stored = packed_rows(size, tables.shape[1], width)[1]
        outs = [jax.ShapeDtypeStruct((stored, width), jnp.bfloat16)]
    if kind == "own":
        outs.append(jax.ShapeDtypeStruct((8, LANES), jnp.float32))
    return pl.pallas_call(
        functools.partial(terms_kernel, kind, cut, segments, stands),
        out_shape=tuple(outs),
        in_specs=[whole(pltpu.SMEM)] * 3 + [whole()] * (2 + len(extra) + len(shards)),
        out_specs=(whole(),) * len(outs),
        scratch_shapes=[
            pltpu.VMEM((2 * QUAD * rows + 8, LANES), jnp.float32),
            pltpu.VMEM((2 * source.shape[0] + 8, LANES), jnp.float32),
        ],
        compiler_params=params(),
        cost_estimate=COST,
        name="terms_" + kind,
    )(source, target, bounds, table_ids, tables, *extra, *shards)


def join_kernel(cuts, count, base_ref, mie_ref, x_ref, sums_in_ref, *rest):
    served, rest = rest[: count * len(cuts)], rest[count * len(cuts) :]
    second = cuts[0][1] < cuts[-1][1]
    if second:
        old, rest = rest[: len(cuts)], rest[len(cuts) :]
    image_ref, *coded, sums_ref = rest
    coefs = base_ref.shape[1]
    width = served[0].shape[1]
    totals = [jnp.zeros((1, 1), jnp.float32)] * 3

    def dot(a, b):
        return jnp.sum(jnp.sum(a * b, axis=0, keepdims=True), axis=1, keepdims=True)

    for k, (start, stop) in enumerate(cuts):
        at = pl.ds(start, stop - start)
        here = served[k * count : (k + 1) * count]
        far_rows = here[0][...].astype(jnp.float32)
        for other in here[1:]:
            far_rows = far_rows + other[...].astype(jnp.float32)
        far_rows = unpack(far_rows, stop - start, coefs)
        image = pad_lanes(base_ref[at, :] + far_rows, width).T[:coefs, :]
        image = mie_ref[:, at] * image
        image_ref[:, pl.ds(start - cuts[0][0], stop - start)] = image
        x = x_ref[:, at]
        if second:
            new = [dot(x, image), dot(old[k][...], image), dot(image, image)]
        else:
            wide = jnp.concatenate([image, jnp.zeros((width - coefs, stop - start), image.dtype)], axis=0)
            coded[0][...] = wide.T.astype(jnp.bfloat16)
            new = [dot(x, image), dot(x, x), dot(image, image)]
        totals = [a + b for a, b in zip(totals, new, strict=True)]
    lane = lax.broadcasted_iota(jnp.int32, (1, LANES), 1)
    packed = sums_in_ref[...]
    for k, total in enumerate(totals):
        packed = packed + jnp.where(lane == k + (3 if second else 0), total, 0.0)
    sums_ref[...] = jnp.broadcast_to(packed, sums_ref.shape)


def join(cuts, base, mie_t, x_t, sums, served, old=(), devices=1):
    rows, coefs = base.shape
    size = cuts[-1][1] - cuts[0][0]
    outs = [jax.ShapeDtypeStruct((coefs, size), jnp.float32)]
    if not old:
        outs.append(jax.ShapeDtypeStruct((size, served[0].shape[1]), jnp.bfloat16))
    outs.append(jax.ShapeDtypeStruct((devices, LANES), jnp.float32))
    return pl.pallas_call(
        functools.partial(join_kernel, cuts, len(served) // len(cuts)),
        out_shape=tuple(outs),
        in_specs=[whole()] * (4 + len(served) + len(old)),
        out_specs=(whole(),) * len(outs),
        compiler_params=params(),
        name="join_second" if old else "join_first",
    )(base, mie_t, x_t, sums, *served, *old)


def finish_kernel(sums_ref, x_ref, c_ref, *rest):
    *parts, solution_ref, residual_ref, hess_ref = rest
    sums = jnp.sum(sums_ref[...], axis=0, keepdims=True)
    xb, xx, bb, xc, bc, cc = [sums[:, k : k + 1] for k in range(6)]
    norm = jnp.sqrt(xx + epsilon)
    inverse = 1.0 / norm
    squared = inverse * inverse
    h11 = (xx - xb) * squared
    g = (xb + epsilon) * squared
    size1 = (g * g * xx - 2.0 * g * xb + bb) * squared
    h21 = jnp.sqrt(jnp.maximum(size1, 0.0) + epsilon)
    q = inverse / h21
    v11 = xx * squared
    v12 = q * inverse * (g * xx - xb)
    v22 = size1 / (h21 * h21)
    p1 = q * inverse * (g * xb - xc)
    p2 = q * q * (g * g * xb - g * xc - g * bb + bc)
    pp = q * q * (g * g * bb - 2.0 * g * bc + cc)
    h12 = v12 - p1
    h22 = v22 - p2
    rest = 1.0 - h22
    size2 = (
        rest * rest * v22
        + h12 * h12 * v11
        + pp
        - 2.0 * rest * h12 * v12
        - 2.0 * rest * p2
        + 2.0 * h12 * p1
    )
    h32 = jnp.sqrt(jnp.maximum(size2, 0.0) + epsilon)
    gram00 = h11 * h11 + h21 * h21
    gram01 = h11 * h12 + h21 * h22
    gram11 = h12 * h12 + h22 * h22 + h32 * h32
    rhs0, rhs1 = norm * h11, norm * h12
    det = gram00 * gram11 - gram01 * gram01
    a1 = (gram11 * rhs0 - gram01 * rhs1) / det * inverse
    a2 = (gram00 * rhs1 - gram01 * rhs0) / det * q
    start = 0
    for b_ref in parts:
        at = pl.ds(start, b_ref.shape[1])
        x, b, c = x_ref[:, at], b_ref[...], c_ref[:, at]
        solution_ref[:, at] = (a1 + a2 * g) * x - a2 * b
        residual_ref[:, at] = (1.0 - a1 - a2 * g) * x + (a1 + a2 * (1.0 + g)) * b - a2 * c
        start += b_ref.shape[1]
    hess_ref[0:1, 0:1] = h11
    hess_ref[0:1, 1:2] = h21
    hess_ref[0:1, 2:3] = jnp.zeros_like(h11)
    hess_ref[1:2, 0:1] = h12
    hess_ref[1:2, 1:2] = h22
    hess_ref[1:2, 2:3] = h32


def finish(sums, x_t, c_t, parts):
    field = jax.ShapeDtypeStruct(x_t.shape, jnp.float32)
    return pl.pallas_call(
        finish_kernel,
        out_shape=(field, field, jax.ShapeDtypeStruct((2, 3), jnp.float32)),
        in_specs=[whole()] * (3 + len(parts)),
        out_specs=(whole(),) * 3,
        compiler_params=params(),
        name="finish",
    )(sums, x_t, c_t, *parts)


def flip(block, bits):
    return lax.ppermute(block, "grp", [(i, i ^ bits) for i in range(lax.axis_size("grp"))])


def once(*values):
    return lax.optimization_barrier(values)


def wave_swaps(waves, count):
    blocks = lax.axis_size("blk")
    while waves.shape[0] < min(count, blocks):
        bits = waves.shape[0]
        moved = lax.ppermute(waves, "blk", [(i, i ^ bits) for i in range(blocks)])
        waves = jnp.concatenate([waves, moved], axis=0)
    return waves


def body(
    incident,
    mie_coef,
    owner_dev,
    near_row,
    table_id,
    tables,
    wave_out,
    wave_in,
    plane_angle,
    far_trans,
):
    x = incident[0]
    mie_t = mie_coef[0].T
    angle = plane_angle[0]
    rows, coefs = x.shape
    width = -(-coefs // LANES) * LANES
    group = lax.axis_size("grp")
    devices = group * lax.axis_size("blk")
    tables_count = tables.shape[0]
    wave_in_t = wave_in.T
    x_t = x.T

    apart = owner_dev[0, :, 0] ^ lax.axis_index("grp")
    count = apart.shape[0]
    bits = (count - 1).bit_length()
    number = jnp.arange(count, dtype=jnp.int32)
    cuts = ((0, rows * 5 // 8), (rows * 5 // 8, rows))
    kind = jnp.where(number < cuts[0][1] * (count // rows), 0, group) + apart
    listed = jnp.sort(((kind * rows + near_row[0]) << bits) | number)
    bounds = jnp.arange(2 * group + 1, dtype=jnp.int32)
    bounds = jnp.sum((kind[None, :] < bounds[:, None]).astype(jnp.int32), axis=1)
    others = range(1, group // QUAD)

    def requests_of(message):
        word = message[:count]
        names = message[count : 2 * count].astype(jnp.bfloat16).reshape(rows, -1)
        source = 2 * ((word >> bits) % (QUAD * rows))
        return source, 2 * (word & ((1 << bits) - 1)), message[2 * count :], names

    message = jnp.concatenate([listed, table_id[0], bounds])
    asked = [flip(message, QUAD * j) for j in others]
    blocks = lax.axis_size("blk")
    turns = jnp.arange(blocks, dtype=jnp.int32)
    weights = far_trans[0, 0][turns ^ lax.axis_index("blk")]
    weights = jnp.where(turns[:, None] > 0, weights, 0.0)

    def incoming_of(waves):
        waves = wave_swaps(waves, blocks)
        return jnp.sum(weights * waves, axis=0, keepdims=True)

    def placed(first, *fields):
        return [
            ((first + place) * rows + start, block)
            for place, field in enumerate(fields)
            for (start, _), block in zip(cuts, field, strict=True)
        ]

    def near_of(shards, incoming):
        segments = ((0, QUAD), (group, group + QUAD))
        return terms("near", (0, rows), segments, shards, local, tables, incoming, wave_in_t, angle)[0]

    def swapped(blocks, bits):
        return [flip(block, bits) for block in blocks]

    coded = code(x_t, width, cuts)
    across, same = swapped(coded, 2), swapped(coded, 1)
    waves = gather_wave(coded, wave_out, angle)
    *across, asked = once(*across, asked)
    asked = [requests_of(words) for words in asked]
    local = requests_of(message)
    beyond = swapped(across, 1)
    shards = placed(0, coded, same, across, beyond)
    served = [
        [
            flip(
                terms(
                    "all",
                    cut,
                    ((part * group + QUAD * j, part * group + QUAD * j + QUAD),),
                    shards,
                    words,
                    tables,
                )[0],
                QUAD * j,
            )
            for j, words in zip(others, asked, strict=True)
        ]
        for part, cut in enumerate(cuts)
    ]
    base = near_of(shards, incoming_of(waves))
    b_t, coded, sums = [], [], jnp.zeros((1, LANES), jnp.float32)
    for cut, arrays in zip(cuts, served, strict=True):
        image, block, sums = join((cut,), base, mie_t, x_t, sums, arrays)
        b_t.append(image)
        coded.append(block)

    across, same = swapped(coded, 2), swapped(coded, 1)
    shards = placed(0, coded, same)
    own = [
        terms(
            "own",
            (0, rows),
            ((QUAD * j, QUAD * j + 2), (group + QUAD * j, group + QUAD * j + 2)),
            shards,
            words,
            tables,
        )
        for j, words in zip(others, asked, strict=True)
    ]
    *across, done = once(*across, [done for _, done in own])
    beyond = swapped(across, 1)
    shards = placed(2, across, beyond)
    served = [
        flip(
            terms(
                "rest",
                cut,
                ((part * group + QUAD * j + 2, part * group + QUAD * j + 4),),
                shards,
                words,
                tables,
                sums_here,
                token,
            )[0],
            QUAD * j,
        )
        for part, cut in enumerate(cuts)
        for j, words, (sums_here, _), token in zip(others, asked, own, done, strict=True)
    ]
    shards = placed(0, coded, same, across, beyond)
    base = near_of(shards, incoming_of(gather_wave(coded, wave_out, angle)))
    c_t, sums = join(cuts, base, mie_t, x_t, sums, served, b_t, devices)
    sums = lax.all_to_all(sums, ("blk", "grp"), 0, 0, tiled=True)
    solution_t, residual_t, hess_t = finish(sums, x_t, c_t, b_t)
    return solution_t.T[None], residual_t.T[None], hess_t.T


def solution(mesh):
    return jax.shard_map(
        body,
        mesh=mesh,
        in_specs=(
            P("blk", "grp", None),
            P("blk", "grp", None),
            P("blk", "grp", None),
            P("blk", "grp"),
            P("blk", "grp"),
            P(),
            P(),
            P(),
            P("blk", "grp", None),
            P("blk", "grp", None, None),
        ),
        out_specs=(P("blk", "grp", None), P("blk", "grp", None), P()),
        check_vma=False,
    )
```
